128 devices in a mesh: slab: 4 (over x), dom: 32 (over y, z, core).
Axes of the slice: x: 4, y: 4, z: 4, core: 2. Of those that a mesh axis runs over, the one named last changes fastest.
Arguments:
- incoming: float32 [4, 8192, 4, 128], P('slab', 'dom'), may hold values from -8 to 65, as said below
- dest: int32 [4, 8192], P('slab', 'dom'), may hold values from 0 to 8191, as said below
- counts: int32 [8, 64, 64], P('slab', 'dom'), may hold values from 0 to 128, as said below
Outputs:
- density: float32 [8, 64, 64, 128], P('slab', 'dom')
- laplace: float32 [8, 64, 64, 128], P('slab', 'dom')
The draws below stay inside these ranges and needn't reach their ends.
Inputs may be any that keep to these rules, and one draw needn't show every extreme that they name: `incoming`: positions lie inside the cell that dest assigns to their block, and slots beyond a cell's count hold positions too. dest holds each cell id of the slab exactly once; every block goes to a domain at most 2 indices away along dom, counted cyclically; from one domain exactly 64 blocks go to each of four domains and none to the others. `counts`: the lowest quarter of the z cells are full.
All inputs are finite; a program needn't handle non-finite values.
Results may differ from the reference program's by a relative error of at most 0.0003.
Values sent between devices are 32-bit elements; how exact they have to be, the bound alone decides.
A program may use at most 64 MiB of HBM per device.

```python
import jax
import jax.numpy as jnp
from jax import lax

SLOTS = 128
LX = 2
LY = 2
LZ = 64
CELL_DEV = 256
CAP = 64
CELLS_SLAB = 8192
NX = 8
NY = 64
NZ = 64
N_SLAB = 4
N_DOM = 32


def block_moves(key):
    slab_keys = jax.random.split(jax.random.fold_in(key, 5), N_SLAB)
    offsets = jax.vmap(jax.random.permutation, in_axes=(0, None))(slab_keys, 5)[:, :4] - 2
    sender = jnp.arange(N_DOM, dtype=jnp.int32)
    quarter = jnp.arange(4, dtype=jnp.int32)
    home_dom = (sender[None, :, None] + offsets[:, None, :]) % N_DOM
    cell_ids = home_dom[..., None] * CELL_DEV + quarter[None, None, :, None] * CAP + jnp.arange(CAP, dtype=jnp.int32)[None, None, None, :]
    cell_ids = cell_ids.reshape(N_SLAB * N_DOM, CELL_DEV)
    shuffle_keys = jax.random.split(jax.random.fold_in(key, 6), N_SLAB * N_DOM)
    orders = jax.vmap(jax.random.permutation, in_axes=(0, None))(shuffle_keys, CELL_DEV)
    cell_ids = jnp.take_along_axis(cell_ids, orders, 1)
    return cell_ids.reshape(N_SLAB, N_DOM * CELL_DEV).astype(jnp.int32)


def draw_dest(key, part):
    return block_moves(jax.random.fold_in(key, 71))


def draw_incoming(key, part):
    cell_ids = block_moves(jax.random.fold_in(key, 71))
    float_key = jax.random.fold_in(key, 11)
    owner = cell_ids // CELL_DEV
    within = cell_ids % CELL_DEV
    grid_x = jnp.arange(N_SLAB, dtype=jnp.int32)[:, None] * LX + within // (LY * LZ)
    grid_y = owner * LY + within // LZ % LY
    grid_z = within % LZ
    corner = jnp.stack([grid_x, grid_y, grid_z], 2).astype(jnp.float32)
    jitter = jax.random.uniform(jax.random.fold_in(float_key, 1), (N_SLAB, CELLS_SLAB, 3, SLOTS), jnp.float32)
    position = corner[..., None] + jitter
    field = jnp.clip(jax.random.normal(jax.random.fold_in(float_key, 4), (N_SLAB, CELLS_SLAB, SLOTS), jnp.float32), -6.0, 6.0)
    return jnp.concatenate([position, field[:, :, None, :]], 2).astype(jnp.float32)


def draw_counts(key, part):
    grid_z = jnp.arange(NZ, dtype=jnp.int32)[None, None, :]
    grid_x = jnp.arange(NX, dtype=jnp.int32)[:, None, None]
    fuller = jax.random.randint(jax.random.fold_in(key, 21), (NX, NY, NZ), 64, 129)
    sparse = jax.random.randint(jax.random.fold_in(key, 22), (NX, NY, NZ), 0, 65)
    column = jnp.where(grid_x < NX // 2, fuller, sparse)
    return jnp.where(grid_z < max(NZ // 4, 1), 128, column).astype(jnp.int32)


def setup_inputs(seed: int = 0) -> dict:
    seeds = jax.random.split(jax.random.key(seed), 4)
    incoming = draw_incoming(jax.random.fold_in(seeds[3], 71), 0)
    dest = draw_dest(jax.random.fold_in(seeds[3], 71), 0)
    counts = draw_counts(jax.random.fold_in(seeds[3], 71), 0)
    return dict(incoming=incoming, dest=dest, counts=counts)


radius_eff = 1.0
radius_min = 0.1
ref_density = 268.0825731

def pair_weights(own_cells, own_mask, far_cells, far_mask, diagonal):
    spread = own_cells[:, 0, :, None] - far_cells[:, 0, None, :]
    distance = spread * spread
    for channel in range(1, 3):
        spread = own_cells[:, channel, :, None] - far_cells[:, channel, None, :]
        distance = distance + spread * spread
    radius = jnp.sqrt(jnp.maximum(distance, radius_min * radius_min))
    weight = jnp.maximum(radius_eff / radius - 1.0, 0.0) * own_mask[:, :, None] * far_mask[:, None, :]
    if diagonal:
        weight = weight * (1.0 - jnp.eye(own_mask.shape[1], dtype=weight.dtype))
    return weight

def scatter_blocks(targets, blocks):
    return jnp.zeros_like(blocks).at[targets].set(blocks)

def reference(incoming, dest, counts):
    arranged = jax.vmap(scatter_blocks)(dest, incoming)
    arranged = arranged.reshape(N_SLAB, N_DOM, LX, LY, LZ, 4, SLOTS)
    arranged = arranged.transpose(0, 2, 1, 3, 4, 5, 6).reshape(NX, NY, NZ, 4, SLOTS)
    filled = counts.astype(incoming.dtype)
    padded = jnp.pad(arranged, ((1, 1), (1, 1), (1, 1), (0, 0), (0, 0)))
    padded_count = jnp.pad(filled, 1)
    slot_index = jnp.arange(SLOTS).astype(incoming.dtype)
    anchor = jnp.zeros((), jnp.int32)

    def one_column(column_id):
        row_x = column_id // NY
        row_y = column_id % NY
        own_cells = lax.dynamic_slice(padded, (row_x + 1, row_y + 1, anchor + 1, anchor, anchor), (1, 1, NZ, 4, SLOTS))[0, 0]
        own_count = lax.dynamic_slice(padded_count, (row_x + 1, row_y + 1, anchor + 1), (1, 1, NZ))[0, 0]
        own_mask = (slot_index[None, :] < own_count[:, None]).astype(incoming.dtype)
        total_n = jnp.zeros((NZ, SLOTS), incoming.dtype)
        total_s = jnp.zeros((NZ, SLOTS), incoming.dtype)
        for shift_x in (-1, 0, 1):
            for shift_y in (-1, 0, 1):
                for shift_z in (-1, 0, 1):
                    far_cells = lax.dynamic_slice(padded, (row_x + 1 + shift_x, row_y + 1 + shift_y, anchor + 1 + shift_z, anchor, anchor), (1, 1, NZ, 4, SLOTS))[0, 0]
                    far_count = lax.dynamic_slice(padded_count, (row_x + 1 + shift_x, row_y + 1 + shift_y, anchor + 1 + shift_z), (1, 1, NZ))[0, 0]
                    far_mask = (slot_index[None, :] < far_count[:, None]).astype(incoming.dtype)
                    weight = pair_weights(own_cells, own_mask, far_cells, far_mask, shift_x == 0 and shift_y == 0 and (shift_z == 0))
                    total_n = total_n + weight.sum(2)
                    total_s = total_s + (weight * far_cells[:, 3, None, :]).sum(2)
        return (total_n, total_s)
    sums_n, sums_s = lax.map(one_column, jnp.arange(NX * NY, dtype=jnp.int32))
    sums_n = sums_n.reshape(NX, NY, NZ, SLOTS)
    sums_s = sums_s.reshape(NX, NY, NZ, SLOTS)
    potential = arranged[:, :, :, 3, :]
    density = sums_n / ref_density
    laplace = (sums_s - potential * sums_n) / ref_density
    return (density, laplace)
```

```python
import functools
import jax, jax.numpy as jnp
from jax import lax
from jax.experimental import pallas as pl
from jax.experimental.pallas import tpu as pltpu
from jax.sharding import PartitionSpec as P

f32, bf16 = jnp.float32, jnp.bfloat16
SENT = 100.0
ZP = 66
ref_density = 268.0825731

OFFS = [(0, 0, 0), (0, 0, 1)] + [(dx, dy, dz) for dx, dy in ((0, 1), (1, -1), (1, 0), (1, 1)) for dz in (-1, 0, 1)]
NT = len(OFFS)


def split3(v):
    h = v.astype(bf16).astype(f32)
    r = v - h
    m = r.astype(bf16).astype(f32)
    return h, m, r - m


def left(h, m, l):
    return [h, h, m, m, h, l]


def right(h, m, l):
    return [h, m, h, m, l, h]


def build_cols(p_ref, row0, col, x0, y0, own_cell, b_ref, f_ref, a_ref, stage, stage_a):
    @pl.loop(0, 8)
    def _(k):
        z0 = k * 8
        rows = pl.ds(pl.multiple_of(row0 + z0, 8), 8)
        x = p_ref[rows, 0:128] - x0
        y = p_ref[rows, 128:256] - y0
        zc = (lax.broadcasted_iota(jnp.int32, (8, 128), 0) + z0).astype(f32) + 0.5
        z = p_ref[rows, 256:384] - zc
        f = p_ref[rows, 384:512]
        f_ref[pl.ds(col * ZP + 1 + z0, 8), :] = f
        one = jnp.ones_like(x)
        sx, sy, sz = split3(x), split3(y), split3(z)
        xy = x * x + y * y
        terms = right(*sx) + right(*sy) + list(split3(xy + z * z)) + [None] + right(*sz) + [one] * 3
        for r, v in enumerate(terms):
            if v is not None:
                stage[pl.ds(r, 8, stride=32), :] = v
        b_ref[pl.ds(pl.multiple_of((col * ZP + 1 + z0) * 32, 32), 256), :] = stage[...].astype(bf16)
        if own_cell is None:
            return
        terms = [-2.0 * v for v in left(*sx)] + [-2.0 * v for v in left(*sy)] + [one] * 3 + [None]
        for s in (-1.0, 0.0, 1.0):
            zs = z - s
            terms += [-2.0 * v for v in left(*split3(zs))] + list(split3(xy + zs * zs))
            terms += (list(split3(f)) if s < 0 else [None] * 3) + [None] * 4
        for r, v in enumerate(terms):
            if v is not None:
                stage_a[pl.ds(r, 8, stride=64), :] = v
        for j in range(8):
            t = stage_a[j * 64:j * 64 + 64, :].T
            a_ref[pl.ds(pl.multiple_of((own_cell + z0 + j) * 128, 128), 128), :] = t.astype(bf16)


def cell_of(cell):
    cx, cy, z = cell // 128, (cell // 64) % 2, cell % 64
    return [((cx + dx) * 4 + cy + 1 + dy) * ZP + 1 + z + dz for dx, dy, dz in OFFS]


def make_d(cell, d_ref, a_ref, b_ref):
    a = a_ref[pl.ds(pl.multiple_of(cell * 128, 128), 128), :]
    zero = jnp.zeros((16, 128), bf16)
    ri = lax.broadcasted_iota(jnp.int32, (16, 128), 0)
    pick = jnp.where((ri >= 9) & (ri < 12), 1.0, 0.0).astype(bf16)
    ws = []
    for (dx, dy, dz), c in zip(OFFS, cell_of(cell)):
        b = b_ref[pl.ds(pl.multiple_of(c * 32, 32), 32), :]
        ws.append(jnp.concatenate([b[:16]] + [b[16:] if k == dz else zero for k in (-1, 0, 1)], 0))
    ws.append(jnp.concatenate([zero, pick, zero, zero], 0))
    for t in range(0, NT + 1, 2):
        w = jnp.concatenate(ws[t:t + 2], 1)
        d_ref[:, 128 * t:128 * t + w.shape[1]] = jnp.dot(a, w, preferred_element_type=f32)


def finish(cell, an_ref, as_ref, n_ref, s_ref):
    n_ref[pl.ds(cell, 1), :] = jnp.sum(an_ref[...].T, axis=0, keepdims=True)
    s_ref[pl.ds(cell, 1), :] = jnp.sum(as_ref[...].T, axis=0, keepdims=True)


def pair_sums(R, cell, d_ref, an_ref, as_ref, f_ref, jn_ref, js_ref):
    if R == 0:
        return
    cs = cell_of(cell)
    fj = [jnp.broadcast_to(f_ref[pl.ds(c, 1), :], (8, 128)) for c in cs]
    f0 = fj[0]
    for v in fj[1:]:
        f0 = f0 + v
    cn = [jnp.full((8, 128), -(R // 8.0), f32) for _ in cs]
    fi0 = d_ref[0:8, 128 * NT:128 * NT + 128]
    for r in range(8, R, 8):
        fi0 = fi0 + d_ref[r:r + 8, 128 * NT:128 * NT + 128]
    cm = [-fi0 for _ in cs]
    for r in range(0, R, 8):
        fi = d_ref[r:r + 8, 128 * NT:128 * NT + 128]
        an = jnp.full((8, 128), -float(NT), f32)
        am = -f0
        for t in range(NT):
            d = d_ref[r:r + 8, 128 * t:128 * t + 128]
            q = jnp.maximum(lax.rsqrt(jnp.maximum(d, 0.01)), 1.0)
            an = an + q
            am = am + q * fj[t]
            if t:
                cn[t] = cn[t] + q
                cm[t] = cm[t] + q * fi
        an_ref[r:r + 8, :] = an
        as_ref[r:r + 8, :] = am
    rows = [pl.ds(pl.multiple_of(c * 8, 8), 8) for c in cs]
    olds = [(jn_ref[rows[t], :], js_ref[rows[t], :]) for t in range(1, NT)]
    for t in range(1, NT):
        jn_ref[rows[t], :] = olds[t - 1][0] + cn[t]
        js_ref[rows[t], :] = olds[t - 1][1] + cm[t]


def tree(v, lo, hi, run):
    if hi - lo == 1:
        run(lo)
        return
    mid = (lo + hi) // 2

    @pl.when(v < mid)
    def _():
        tree(v, lo, mid, run)

    @pl.when(v >= mid)
    def _():
        tree(v, mid, hi, run)


def kern(MODE, sc_ref, cnt_ref, home, hy, hm, hx, hxp, hxm, n_ref, s_ref, hs_ref,
         a_ref, b_ref, f_ref, jn_ref, js_ref, stage, stage_a, d0, d1, an0, as0, an1, as1):
    x0 = sc_ref[0]
    y0 = sc_ref[1]
    stage[...] = jnp.zeros_like(stage)
    stage_a[...] = jnp.zeros_like(stage_a)
    ri = lax.broadcasted_iota(jnp.int32, (32, 128), 0)
    rim = (jnp.where(ri == 12, SENT * SENT, 0.0) + jnp.where((ri >= 22) & (ri < 25), 1.0, 0.0)).astype(bf16)

    @pl.loop(0, 12)
    def _(col):
        for zz in (0, ZP - 1):
            b_ref[pl.ds(pl.multiple_of((col * ZP + zz) * 32, 32), 32), :] = rim
            f_ref[pl.ds(col * ZP + zz, 1), :] = jnp.zeros((1, 128), f32)

    @pl.loop(0, 12 * ZP)
    def _(k):
        rows = pl.ds(pl.multiple_of(k * 8, 8), 8)
        jn_ref[rows, :] = jnp.zeros((8, 128), f32)
        js_ref[rows, :] = jnp.zeros((8, 128), f32)

    b = functools.partial(build_cols, x0=x0, y0=y0, b_ref=b_ref, f_ref=f_ref, a_ref=a_ref, stage=stage, stage_a=stage_a)

    @pl.loop(0, 4)
    def _(k):
        b(home, k * 64, (k // 2) * 4 + k % 2 + 1, own_cell=k * 64)

    @pl.loop(0, 2)
    def _(k):
        b(hy, k * 64, k * 4 + 3, own_cell=None)
        b(hx, k * 64, 9 + k, own_cell=None)
    b(hm, 0, 4, own_cell=None)
    b(hxp, 0, 11, own_cell=None)
    b(hxm, 0, 8, own_cell=None)

    if MODE == "build":
        n_ref[...] = jnp.zeros_like(n_ref)
        s_ref[...] = jnp.zeros_like(s_ref)
        hs_ref[...] = jnp.zeros_like(hs_ref)
        return
    make_d(0, d0, a_ref, b_ref)
    bufs = ((d0, an0, as0), (d1, an1, as1))

    @pl.loop(0, 128)
    def _(i):
        for p in range(2):
            cell = i * 2 + p
            nxt = jnp.minimum(cell + 1, 255)
            prev = jnp.maximum(cell - 1, 0)
            d, an, am = bufs[p]
            dn, anp, amp = bufs[1 - p]

            def run(k):
                if MODE != "nod":
                    make_d(nxt, dn, a_ref, b_ref)
                if MODE != "nofin":
                    finish(prev, anp, amp, n_ref, s_ref)
                if MODE != "nopair":
                    pair_sums(16 * k, cell, d, an, am, f_ref, jn_ref, js_ref)
            tree((cnt_ref[cell] + 15) // 16, 0, 9, run)
    finish(255, an1, as1, n_ref, s_ref)

    def side(col, z0, ref):
        base = (col * ZP + 1 + z0) * 8
        v = ref[pl.ds(base, 8, stride=8), :]
        for k in range(1, 8):
            v = v + ref[pl.ds(base + k, 8, stride=8), :]
        return v

    @pl.loop(0, 32)
    def _(k):
        cx, cy, z0 = k // 16, (k // 8) % 2, (k % 8) * 8
        rows = pl.ds(pl.multiple_of(k * 8, 8), 8)
        n_ref[rows, :] += side(cx * 4 + cy + 1, z0, jn_ref)
        s_ref[rows, :] += side(cx * 4 + cy + 1, z0, js_ref)

    @pl.loop(0, 8)
    def _(k):
        for h, col in enumerate((3, 7, 4, 9, 10, 11, 8)):
            rows = pl.ds(pl.multiple_of(h * 64 + k * 8, 8), 8)
            hs_ref[rows, 0:128] = side(col, k * 8, jn_ref)
            hs_ref[rows, 128:256] = side(col, k * 8, js_ref)


def compute(sc, cnt, home, hy, hm, hx, hxp, hxm, MODE="full"):
    vm = pl.BlockSpec(memory_space=pltpu.VMEM)
    sm = pl.BlockSpec(memory_space=pltpu.SMEM)
    return pl.pallas_call(
        functools.partial(kern, MODE),
        out_shape=[jax.ShapeDtypeStruct((256, 128), f32)] * 2 + [jax.ShapeDtypeStruct((448, 256), f32)],
        in_specs=[sm, sm] + [vm] * 6, out_specs=[vm] * 3,
        scratch_shapes=[pltpu.VMEM((256 * 128, 64), bf16), pltpu.VMEM((12 * ZP * 32, 128), bf16),
                        pltpu.VMEM((12 * ZP, 128), f32), pltpu.VMEM((12 * ZP * 8, 128), f32), pltpu.VMEM((12 * ZP * 8, 128), f32),
                        pltpu.VMEM((256, 128), f32), pltpu.VMEM((512, 128), f32)]
        + [pltpu.VMEM((128, 128 * (NT + 1)), f32)] * 2 + [pltpu.VMEM((128, 128), f32)] * 4,
        compiler_params=pltpu.CompilerParams(vmem_limit_bytes=56 * 2**20),
        name="pairs",
    )(sc, cnt, home, hy, hm, hx, hxp, hxm)


def turned(value, axes, step):
    size = (lax.axis_size("slab"), lax.axis_size("dom"))
    if len(axes) == 1:
        count = lax.axis_size(axes[0])
        return lax.ppermute(value, axes[0], [(i, (i + step[0]) % count) for i in range(count)])
    pairs = []
    for s in range(size[0]):
        for d in range(size[1]):
            pairs.append((s * size[1] + d, (s + step[0]) % size[0] * size[1] + (d + step[1]) % size[1]))
    return lax.ppermute(value, axes, pairs)


def local(incoming, dest, counts):
    cells = 256
    blocks = incoming.reshape(cells, 512)
    targets = dest.reshape(cells)
    me = lax.axis_index("dom")
    shift = (targets // cells - me + 2) % 32
    chosen = (shift[None, :] == jnp.arange(5)[:, None]).astype(f32)
    lower = (jnp.arange(cells)[:, None] <= jnp.arange(cells)[None, :]).astype(f32)
    rank = jnp.sum(jnp.dot(chosen, lower) * chosen, 0) - 1.0
    slot = shift.astype(f32) * 64.0 + rank
    pack = (jnp.arange(320, dtype=f32)[:, None] == slot[None, :]).astype(f32)
    tag = jnp.broadcast_to((targets % cells + 1).astype(f32)[:, None], (cells, 128))
    packed = jnp.dot(pack, jnp.concatenate([blocks, tag], 1), precision=lax.Precision.HIGHEST)
    got = [turned(packed[64 * k:64 * k + 64], ("dom",), (k - 2,)) if k != 2 else packed[128:192] for k in range(5)]
    got = jnp.concatenate(got, 0)
    place = (jnp.arange(cells, dtype=f32)[:, None] + 1.0 == got[None, :, 512]).astype(f32)
    home = jnp.dot(place, got[:, :512], precision=lax.Precision.HIGHEST)
    count = counts.reshape(cells)
    filled = jnp.arange(128)[None, :] < count[:, None]
    x0 = (lax.axis_index("slab") * 2 + 1).astype(f32)
    y0 = (me * 2 + 1).astype(f32)
    home = jnp.concatenate(
        [jnp.where(filled, home[:, :128], x0 + SENT), home[:, 128:384], jnp.where(filled, home[:, 384:], 0.0)], 1)
    both = ("slab", "dom")
    hy = turned(jnp.concatenate([home[0:64], home[128:192]], 0), ("dom",), (-1,))
    hm = turned(home[192:256], ("dom",), (1,))
    hx = turned(home[0:128], ("slab",), (-1,))
    hxp = turned(home[0:64], both, (-1, -1))
    hxm = turned(home[64:128], both, (-1, 1))
    n, s, hs = compute(jnp.stack([x0, y0]), count, home, hy, hm, hx, hxp, hxm)
    by = turned(hs[0:128], ("dom",), (1,))
    bm = turned(hs[128:192], ("dom",), (-1,))
    bx = turned(hs[192:320], ("slab",), (1,))
    bxp = turned(hs[320:384], both, (1, 1))
    bxm = turned(hs[384:448], both, (1, -1))
    back = jnp.concatenate([by[:64] + bx[:64] + bxp, bx[64:] + bxm, by[64:], bm], 0)
    n = n + back[:, :128]
    s = s + back[:, 128:]
    own = lax.rsqrt(jnp.full((), 0.01, f32)) - 1.0
    density = jnp.where(filled, (n - own) / ref_density, 0.0)
    laplace = jnp.where(filled, (s - home[:, 384:] * n) / ref_density, 0.0)
    return density.reshape(2, 2, 64, 128), laplace.reshape(2, 2, 64, 128)


def solution(mesh):
    in_specs = (P("slab", "dom", None, None), P("slab", "dom"), P("slab", "dom", None))
    out_specs = (P("slab", "dom", None, None), P("slab", "dom", None, None))
    return jax.shard_map(local, mesh=mesh, in_specs=in_specs, out_specs=out_specs, check_vma=False)
```

```python
import functools
import jax, jax.numpy as jnp
from jax import lax
from jax.experimental import pallas as pl
from jax.experimental.pallas import tpu as pltpu
from jax.sharding import PartitionSpec as P

f32, bf16 = jnp.float32, jnp.bfloat16
SENT = 100.0
ZP = 66
ref_density = 268.0825731
N_SLAB, N_DOM = 4, 32

OFFS = [(0, 0, 0), (0, 0, 1)] + [(dx, dy, dz) for dx, dy in ((0, 1), (1, -1), (1, 0), (1, 1)) for dz in (-1, 0, 1)]
NT = len(OFFS)
FR = 4


def split3(v):
    h = v.astype(bf16).astype(f32)
    r = v - h
    m = r.astype(bf16).astype(f32)
    return h, m, r - m


def left(h, m, l):
    return [h, h, m, m, h, l]


def right(h, m, l):
    return [h, m, h, m, l, h]


def build_cols(p_ref, row0, col, x0, y0, own_cell, b_ref, f_ref, a_ref, stage, stage_a):
    @pl.loop(0, 8)
    def _(k):
        z0 = k * 8
        rows = pl.ds(pl.multiple_of(row0 + z0, 8), 8)
        x = p_ref[rows, 0:128] - x0
        y = p_ref[rows, 128:256] - y0
        zc = (lax.broadcasted_iota(jnp.int32, (8, 128), 0) + z0).astype(f32) + 0.5
        z = p_ref[rows, 256:384] - zc
        f = p_ref[rows, 384:512]
        f_ref[pl.ds(col * ZP + 1 + z0, 8), :] = f
        one = jnp.ones_like(x)
        sx, sy, sz = split3(x), split3(y), split3(z)
        xy = x * x + y * y
        terms = right(*sx) + right(*sy) + list(split3(xy + z * z)) + [None] + right(*sz) + [one] * 3
        for r, v in enumerate(terms):
            if v is not None:
                stage[pl.ds(r, 8, stride=32), :] = v
        b_ref[pl.ds(pl.multiple_of((col * ZP + 1 + z0) * 32, 32), 256), :] = stage[...].astype(bf16)
        if own_cell is None:
            return
        terms = [-2.0 * v for v in left(*sx)] + [-2.0 * v for v in left(*sy)] + [one] * 3 + [None]
        for s in (-1.0, 0.0, 1.0):
            zs = z - s
            terms += [-2.0 * v for v in left(*split3(zs))] + list(split3(xy + zs * zs))
            terms += (list(split3(f)) if s < 0 else [None] * 3) + [None] * 4
        for r, v in enumerate(terms):
            if v is not None:
                stage_a[pl.ds(r, 8, stride=64), :] = v
        for j in range(8):
            t = stage_a[j * 64:j * 64 + 64, :].T
            a_ref[pl.ds(pl.multiple_of((own_cell + z0 + j) * 128, 128), 128), :] = t.astype(bf16)


def cell_of(cell):
    cx, cy, z = cell // 128, (cell // 64) % 2, cell % 64
    return [((cx + dx) * 4 + cy + 1 + dy) * ZP + 1 + z + dz for dx, dy, dz in OFFS]


def make_d(cell, d_ref, a_ref, b_ref):
    a = a_ref[pl.ds(pl.multiple_of(cell * 128, 128), 128), :]
    zero = jnp.zeros((16, 128), bf16)
    ri = lax.broadcasted_iota(jnp.int32, (16, 128), 0)
    pick = jnp.where((ri >= 9) & (ri < 12), 1.0, 0.0).astype(bf16)
    ws = []
    for (dx, dy, dz), c in zip(OFFS, cell_of(cell)):
        b = b_ref[pl.ds(pl.multiple_of(c * 32, 32), 32), :]
        ws.append(jnp.concatenate([b[:16]] + [b[16:] if k == dz else zero for k in (-1, 0, 1)], 0))
    ws.append(jnp.concatenate([zero, pick, zero, zero], 0))

    def part(t):
        w = jnp.concatenate(ws[t:t + 2], 1)
        d_ref[:, 128 * t:128 * t + w.shape[1]] = jnp.dot(a, w, preferred_element_type=f32)
    return [functools.partial(part, t) for t in range(0, NT + 1, 2)]


def finish(cell, an_ref, as_ref, n_ref, s_ref):
    n_ref[pl.ds(cell, 1), :] = jnp.sum(an_ref[...].T, axis=0, keepdims=True)
    s_ref[pl.ds(cell, 1), :] = jnp.sum(as_ref[...].T, axis=0, keepdims=True)


def pair_sums(R, cell, d_ref, an_ref, as_ref, f_ref, jn_ref, js_ref, parts):
    if R == 0:
        for part in parts:
            part()
        return
    cs = cell_of(cell)
    fj = [jnp.broadcast_to(f_ref[pl.ds(c, 1), :], (8, 128)) for c in cs]
    f0 = fj[0]
    for v in fj[1:]:
        f0 = f0 + v
    cn = [jnp.full((8, 128), -(R // 8.0), f32) for _ in cs]
    fi0 = d_ref[0:8, 128 * NT:128 * NT + 128]
    for r in range(8, R, 8):
        fi0 = fi0 + d_ref[r:r + 8, 128 * NT:128 * NT + 128]
    cm = [-fi0 for _ in cs]
    for r in range(0, R, 8):
        fi = d_ref[r:r + 8, 128 * NT:128 * NT + 128]
        an = jnp.full((8, 128), -float(NT), f32)
        am = -f0
        for t in range(NT):
            d = d_ref[r:r + 8, 128 * t:128 * t + 128]
            q = jnp.maximum(lax.rsqrt(jnp.maximum(d, 0.01)), 1.0)
            an = an + q
            am = am + q * fj[t]
            if t:
                cn[t] = cn[t] + q
                cm[t] = cm[t] + q * fi
        an_ref[r:r + 8, :] = an
        as_ref[r:r + 8, :] = am
        for part in parts[min(FR * r * len(parts) // R // 4, len(parts)):min(FR * (r + 8) * len(parts) // R // 4, len(parts))]:
            part()
    rows = [pl.ds(pl.multiple_of(c * 8, 8), 8) for c in cs]
    olds = [(jn_ref[rows[t], :], js_ref[rows[t], :]) for t in range(1, NT)]
    for t in range(1, NT):
        jn_ref[rows[t], :] = olds[t - 1][0] + cn[t]
        js_ref[rows[t], :] = olds[t - 1][1] + cm[t]


def tree(v, lo, hi, run):
    if hi - lo == 1:
        run(lo)
        return
    mid = (lo + hi) // 2

    @pl.when(v < mid)
    def _():
        tree(v, lo, mid, run)

    @pl.when(v >= mid)
    def _():
        tree(v, mid, hi, run)


def kern(MODE, sc_ref, cnt_ref, home, hy, hm, hx, hxp, hxm, n_ref, s_ref, hs_ref,
         a_ref, b_ref, f_ref, jn_ref, js_ref, stage, stage_a, d0, d1, an0, as0, an1, as1):
    x0 = sc_ref[0]
    y0 = sc_ref[1]
    stage[...] = jnp.zeros_like(stage)
    stage_a[...] = jnp.zeros_like(stage_a)
    ri = lax.broadcasted_iota(jnp.int32, (32, 128), 0)
    rim = (jnp.where(ri == 12, SENT * SENT, 0.0) + jnp.where((ri >= 22) & (ri < 25), 1.0, 0.0)).astype(bf16)

    @pl.loop(0, 12)
    def _(col):
        for zz in (0, ZP - 1):
            b_ref[pl.ds(pl.multiple_of((col * ZP + zz) * 32, 32), 32), :] = rim
            f_ref[pl.ds(col * ZP + zz, 1), :] = jnp.zeros((1, 128), f32)

    @pl.loop(0, 12 * ZP)
    def _(k):
        rows = pl.ds(pl.multiple_of(k * 8, 8), 8)
        jn_ref[rows, :] = jnp.zeros((8, 128), f32)
        js_ref[rows, :] = jnp.zeros((8, 128), f32)

    b = functools.partial(build_cols, x0=x0, y0=y0, b_ref=b_ref, f_ref=f_ref, a_ref=a_ref, stage=stage, stage_a=stage_a)

    @pl.loop(0, 4)
    def _(k):
        b(home, k * 64, (k // 2) * 4 + k % 2 + 1, own_cell=k * 64)

    @pl.loop(0, 2)
    def _(k):
        b(hy, k * 64, k * 4 + 3, own_cell=None)
        b(hx, k * 64, 9 + k, own_cell=None)
    b(hm, 0, 4, own_cell=None)
    b(hxp, 0, 11, own_cell=None)
    b(hxm, 0, 8, own_cell=None)

    if MODE == "build":
        n_ref[...] = jnp.zeros_like(n_ref)
        s_ref[...] = jnp.zeros_like(s_ref)
        hs_ref[...] = jnp.zeros_like(hs_ref)
        return
    for part in make_d(0, d0, a_ref, b_ref):
        part()
    bufs = ((d0, an0, as0), (d1, an1, as1))

    @pl.loop(0, 128)
    def _(i):
        for p in range(2):
            cell = i * 2 + p
            nxt = jnp.minimum(cell + 1, 255)
            prev = jnp.maximum(cell - 1, 0)
            d, an, am = bufs[p]
            dn, anp, amp = bufs[1 - p]

            def run(k):
                parts = make_d(nxt, dn, a_ref, b_ref)
                if MODE != "nofin":
                    finish(prev, anp, amp, n_ref, s_ref)
                if MODE != "nopair":
                    pair_sums(16 * k, cell, d, an, am, f_ref, jn_ref, js_ref, parts)
            tree((cnt_ref[cell] + 15) // 16, 0, 9, run)
    finish(255, an1, as1, n_ref, s_ref)

    def side(col, z0, ref):
        base = (col * ZP + 1 + z0) * 8
        v = ref[pl.ds(base, 8, stride=8), :]
        for k in range(1, 8):
            v = v + ref[pl.ds(base + k, 8, stride=8), :]
        return v

    @pl.loop(0, 32)
    def _(k):
        cx, cy, z0 = k // 16, (k // 8) % 2, (k % 8) * 8
        rows = pl.ds(pl.multiple_of(k * 8, 8), 8)
        n_ref[rows, :] += side(cx * 4 + cy + 1, z0, jn_ref)
        s_ref[rows, :] += side(cx * 4 + cy + 1, z0, js_ref)

    @pl.loop(0, 8)
    def _(k):
        for h, col in enumerate((3, 7, 4, 9, 10, 11, 8)):
            rows = pl.ds(pl.multiple_of(h * 64 + k * 8, 8), 8)
            hs_ref[rows, 0:128] = side(col, k * 8, jn_ref)
            hs_ref[rows, 128:256] = side(col, k * 8, js_ref)


def compute(sc, cnt, home, hy, hm, hx, hxp, hxm, MODE="full"):
    vm = pl.BlockSpec(memory_space=pltpu.VMEM)
    sm = pl.BlockSpec(memory_space=pltpu.SMEM)
    return pl.pallas_call(
        functools.partial(kern, MODE),
        out_shape=[jax.ShapeDtypeStruct((256, 128), f32)] * 2 + [jax.ShapeDtypeStruct((448, 256), f32)],
        in_specs=[sm, sm] + [vm] * 6, out_specs=[vm] * 3,
        scratch_shapes=[pltpu.VMEM((256 * 128, 64), bf16), pltpu.VMEM((12 * ZP * 32, 128), bf16),
                        pltpu.VMEM((12 * ZP, 128), f32), pltpu.VMEM((12 * ZP * 8, 128), f32), pltpu.VMEM((12 * ZP * 8, 128), f32),
                        pltpu.VMEM((256, 128), f32), pltpu.VMEM((512, 128), f32)]
        + [pltpu.VMEM((128, 128 * (NT + 1)), f32)] * 2 + [pltpu.VMEM((128, 128), f32)] * 4,
        compiler_params=pltpu.CompilerParams(vmem_limit_bytes=56 * 2**20),
        name="pairs",
    )(sc, cnt, home, hy, hm, hx, hxp, hxm)


def far(ds, dd):
    slab = lax.rem(lax.axis_index("slab") + (ds + N_SLAB), N_SLAB)
    dom = lax.rem(lax.axis_index("dom") + (dd + N_DOM), N_DOM)
    return (slab, dom)


def copy_to(src, dst, send, recv, where):
    return pltpu.make_async_remote_copy(
        src_ref=src, dst_ref=dst, send_sem=send, recv_sem=recv, device_id=far(*where),
        device_id_type=pl.DeviceIdType.MESH)


def greet(senders):
    barrier = pltpu.get_barrier_semaphore()
    for where in senders:
        pl.semaphore_signal(barrier, inc=1, device_id=far(*where), device_id_type=pl.DeviceIdType.MESH)
    pl.semaphore_wait(barrier, len(senders))


def picked(onehot, v, dims):
    out = None
    for part in reversed(split3(v)):
        p = lax.dot_general(onehot, part.astype(bf16), (dims, ((), ())), preferred_element_type=f32)
        out = p if out is None else out + p
    return out


def iota(shape, dim):
    return lax.broadcasted_iota(jnp.int32, shape, dim).astype(f32)


FAR = (0, 4, 1, 3)
HALO = ((0, 64, (0, -1), 0, 0), (128, 64, (0, -1), 0, 64), (192, 64, (0, 1), 1, 0), (0, 128, (-1, 0), 2, 0),
        (0, 64, (-1, -1), 3, 0), (64, 64, (-1, 1), 4, 0))


def relayout_kernel(x_ref, dest_ref, cnt_ref, home, hy, hm, hx, hxp, hxm, sent, got, s1, r1, s2, r2):
    me = lax.axis_index("dom")
    greet([(0, -2), (0, -1), (0, 1), (0, 2), (1, 0), (1, 1), (1, -1)])
    dest = dest_ref[...]
    dom = lax.shift_right_logical(dest, 8)
    shift = (dom - me).astype(f32)
    shift = jnp.where(shift < -16.0, shift + 32.0, jnp.where(shift > 16.0, shift - 32.0, shift)) + 2.0
    local = (dest - dom * 256).astype(f32)
    chosen = jnp.where(iota((8, 256), 0) == shift, 1.0, 0.0)
    lower = jnp.where(iota((256, 256), 0) <= iota((256, 256), 1), 1.0, 0.0).astype(bf16)
    rank = jnp.dot(chosen.astype(bf16), lower, preferred_element_type=f32)
    rank = jnp.sum(chosen * rank, axis=0, keepdims=True) - 1.0
    slot = shift * 64.0 + rank
    xs = [x_ref[:, c, :] for c in range(4)]
    diag = jnp.where(iota((256, 256), 0) == iota((256, 256), 1), 1.0, 0.0)
    tag = jnp.broadcast_to(jnp.sum(diag * local, axis=1, keepdims=True) + 1.0, (256, 128))
    data = jnp.concatenate(xs, 1)
    first = []
    for k in FAR:
        pack = jnp.where(iota((64, 256), 0) + 64.0 * k == slot, 1.0, 0.0).astype(bf16)
        sent[k, :, 0:512] = picked(pack, data, ((1,), (0,)))
        sent[k, :, 512:640] = jnp.dot(pack, tag.astype(bf16), preferred_element_type=f32)
        c = copy_to(sent.at[k], got.at[k], s1.at[k], r1.at[k], (0, k - 2))
        c.start()
        first.append(c)
    pack = jnp.where(iota((64, 256), 0) + 128.0 == slot, 1.0, 0.0).astype(bf16)
    got[2, :, 0:512] = picked(pack, data, ((1,), (0,)))
    got[2, :, 512:640] = jnp.dot(pack, tag.astype(bf16), preferred_element_type=f32)
    count = jnp.sum(diag * cnt_ref[...].astype(f32), axis=1, keepdims=True)
    filled = iota((256, 128), 1) < count
    total = None
    for k in (2,) + FAR[::-1]:
        if k != 2:
            first[FAR.index(k)].wait_recv()
        label = got[k, :, 512:640]
        lanes = iota((64, 128), 1)
        place = jnp.concatenate([jnp.where(label == lanes + 1.0, 1.0, 0.0), jnp.where(label == lanes + 129.0, 1.0, 0.0)], 1)
        part = picked(place.T.astype(bf16), got[k, :, 0:512], ((1,), (0,)))
        total = part if total is None else total + part
    x0 = (lax.axis_index("slab") * 2 + 1).astype(f32)
    home[:, 0:128] = jnp.where(filled, total[:, 0:128], x0 + SENT)
    home[:, 128:384] = total[:, 128:384]
    home[:, 384:512] = jnp.where(filled, total[:, 384:512], 0.0)
    outs = (hy, hm, hx, hxp, hxm)
    second = []
    for k, (row, rows, where, o, there) in enumerate(HALO):
        c = copy_to(home.at[pl.ds(row, rows)], outs[o].at[pl.ds(there, rows)], s2.at[k], r2.at[k], where)
        c.start()
        second.append(c)
    for c in first:
        c.wait_send()
    for c in second:
        c.wait()


def relayout(x, dest, count):
    vm = pl.BlockSpec(memory_space=pltpu.VMEM)
    return pl.pallas_call(
        relayout_kernel,
        out_shape=[jax.ShapeDtypeStruct((r, 512), f32) for r in (256, 128, 64, 128, 64, 64)],
        in_specs=[vm] * 3, out_specs=[vm] * 6,
        scratch_shapes=[pltpu.VMEM((5, 64, 640), f32)] * 2
        + [pltpu.SemaphoreType.DMA((5,))] * 2 + [pltpu.SemaphoreType.DMA((6,))] * 2,
        compiler_params=pltpu.CompilerParams(collective_id=0, has_side_effects=True, vmem_limit_bytes=32 * 2**20),
        name="relayout",
    )(x, dest, count)


BACK = ((0, 128, (0, 1)), (128, 64, (0, -1)), (192, 128, (1, 0)), (320, 64, (1, 1)), (384, 64, (1, -1)))


def combine_kernel(n_ref, s_ref, hs, home, cnt_ref, dens, lap, got, s1, r1):
    greet([(0, -1), (0, 1), (-1, 0), (-1, -1), (-1, 1)])
    copies = []
    for k, (row, rows, where) in enumerate(BACK):
        part = pl.ds(row, rows)
        c = copy_to(hs.at[part], got.at[part], s1.at[k], r1.at[k], where)
        c.start()
        copies.append(c)
    diag = jnp.where(iota((256, 256), 0) == iota((256, 256), 1), 1.0, 0.0)
    count = jnp.sum(diag * cnt_ref[...].astype(f32), axis=1, keepdims=True)
    for c in copies:
        c.wait()
    own = lax.rsqrt(jnp.full((64, 128), 0.01, f32)) - 1.0
    lists = ((0, 192, 320), (256, 384), (64,), (128,))
    for q in range(4):
        rows = slice(64 * q, 64 * q + 64)
        n = n_ref[rows, :]
        s = s_ref[rows, :]
        for r in lists[q]:
            n = n + got[r:r + 64, 0:128]
            s = s + got[r:r + 64, 128:256]
        filled = iota((64, 128), 1) < count[rows]
        dens[rows, :] = jnp.where(filled, (n - own) / ref_density, 0.0)
        lap[rows, :] = jnp.where(filled, (s - home[rows, 384:512] * n) / ref_density, 0.0)


def combine(n, s, hs, home, count):
    vm = pl.BlockSpec(memory_space=pltpu.VMEM)
    return pl.pallas_call(
        combine_kernel,
        out_shape=[jax.ShapeDtypeStruct((256, 128), f32)] * 2,
        in_specs=[vm] * 5, out_specs=[vm] * 2,
        scratch_shapes=[pltpu.VMEM((448, 256), f32), pltpu.SemaphoreType.DMA((5,)), pltpu.SemaphoreType.DMA((5,))],
        compiler_params=pltpu.CompilerParams(collective_id=1, has_side_effects=True, vmem_limit_bytes=16 * 2**20),
        name="combine",
    )(n, s, hs, home, count)


def local(incoming, dest, counts):
    count = counts.reshape(256)
    x0 = (lax.axis_index("slab") * 2 + 1).astype(f32)
    y0 = (lax.axis_index("dom") * 2 + 1).astype(f32)
    home, hy, hm, hx, hxp, hxm = relayout(incoming.reshape(256, 4, 128), dest, count.reshape(1, 256))
    n, s, hs = compute(jnp.stack([x0, y0]), count, home, hy, hm, hx, hxp, hxm)
    density, laplace = combine(n, s, hs, home, count.reshape(1, 256))
    return density.reshape(2, 2, 64, 128), laplace.reshape(2, 2, 64, 128)


def solution(mesh):
    in_specs = (P("slab", "dom", None, None), P("slab", "dom"), P("slab", "dom", None))
    out_specs = (P("slab", "dom", None, None), P("slab", "dom", None, None))
    return jax.shard_map(local, mesh=mesh, in_specs=in_specs, out_specs=out_specs, check_vma=False)
```

```python
import functools
import jax, jax.numpy as jnp
from jax import lax
from jax.experimental import pallas as pl
from jax.experimental.pallas import tpu as pltpu
from jax.sharding import PartitionSpec as P

f32, bf16 = jnp.float32, jnp.bfloat16
SENT = 100.0
ZP = 66
ref_density = 268.0825731
N_SLAB, N_DOM = 4, 32

OFFS = [(0, 0, 0), (0, 0, 1)] + [(dx, dy, dz) for dx, dy in ((0, 1), (1, -1), (1, 0), (1, 1)) for dz in (-1, 0, 1)]
NT = len(OFFS)
FR = 5


def split3(v):
    h = v.astype(bf16).astype(f32)
    r = v - h
    m = r.astype(bf16).astype(f32)
    return h, m, r - m


def split2(v):
    h = v.astype(bf16).astype(f32)
    m = (v - h).astype(bf16).astype(f32)
    return h, m, h + m


def left(h, m):
    return [-2.0 * h, -2.0 * h, -2.0 * m, -2.0 * m]


def right(h, m):
    return [h, m, h, m]


def build_cols(p_ref, row0, col, x0, y0, own_cell, b_ref, f_ref, a_ref, stage, stage_a):
    @pl.loop(0, 8)
    def _(k):
        z0 = k * 8
        rows = pl.ds(pl.multiple_of(row0 + z0, 8), 8)
        zc = (lax.broadcasted_iota(jnp.int32, (8, 128), 0) + z0).astype(f32) + 0.5
        xh, xm, x = split2(p_ref[rows, 0:128] - x0)
        yh, ym, y = split2(p_ref[rows, 128:256] - y0)
        zh, zm, z = split2(p_ref[rows, 256:384] - zc)
        f = p_ref[rows, 384:512]
        f_ref[pl.ds(col * ZP + 1 + z0, 8), :] = f
        xy = x * x + y * y
        terms = dict(enumerate(right(xh, xm) + right(yh, ym) + list(split3(xy + z * z))))
        terms.update(enumerate(right(zh, zm), 16))
        for r, v in terms.items():
            stage[pl.ds(r, 8, stride=32), :] = v
        b_ref[pl.ds(pl.multiple_of((col * ZP + 1 + z0) * 32, 32), 256), :] = stage[...].astype(bf16)
        if own_cell is None:
            return
        terms = dict(enumerate(left(xh, xm) + left(yh, ym)))
        for k2, s in enumerate((-1.0, 0.0, 1.0)):
            h, m, zs = split2(z - s)
            terms.update(enumerate(left(h, m) + list(split3(xy + zs * zs)), 16 + 16 * k2))
        terms.update(enumerate(split3(f), 23))
        for r, v in terms.items():
            stage_a[pl.ds(r, 8, stride=64), :] = v
        for j in range(8):
            t = stage_a[j * 64:j * 64 + 64, :].T
            a_ref[pl.ds(pl.multiple_of((own_cell + z0 + j) * 128, 128), 128), :] = t.astype(bf16)


def cell_of(cell):
    cx, cy, z = cell // 128, (cell // 64) % 2, cell % 64
    return [((cx + dx) * 4 + cy + 1 + dy) * ZP + 1 + z + dz for dx, dy, dz in OFFS]


def make_d(cell, d_ref, a_ref, b_ref):
    a = a_ref[pl.ds(pl.multiple_of(cell * 128, 128), 128), :]
    zero = jnp.zeros((16, 128), bf16)
    ri = lax.broadcasted_iota(jnp.int32, (16, 128), 0)
    pick = jnp.where((ri >= 7) & (ri < 10), 1.0, 0.0).astype(bf16)
    ws = []
    for (dx, dy, dz), c in zip(OFFS, cell_of(cell)):
        b = b_ref[pl.ds(pl.multiple_of(c * 32, 32), 32), :]
        ws.append(jnp.concatenate([b[:16]] + [b[16:] if k == dz else zero for k in (-1, 0, 1)], 0))
    ws.append(jnp.concatenate([zero, pick, zero, zero], 0))

    def part(t, r):
        w = jnp.concatenate(ws[t:t + 2], 1)
        d_ref[r:r + 32, 128 * t:128 * t + w.shape[1]] = jnp.dot(a[r:r + 32], w, preferred_element_type=f32)
    return [functools.partial(part, t, r) for t in range(0, NT + 1, 2) for r in range(0, 128, 32)]


def finish(cell, an_ref, as_ref, out_ref):
    out_ref[0, pl.ds(cell, 1), :] = jnp.sum(an_ref[...].T, axis=0, keepdims=True)
    out_ref[1, pl.ds(cell, 1), :] = jnp.sum(as_ref[...].T, axis=0, keepdims=True)


def pair_sums(R, cell, d_ref, an_ref, as_ref, f_ref, jn_ref, js_ref, parts):
    if R == 0:
        for part in parts:
            part()
        return
    cs = cell_of(cell)
    fj = [jnp.broadcast_to(f_ref[pl.ds(c, 1), :], (8, 128)) for c in cs]
    f0 = fj[0]
    for v in fj[1:]:
        f0 = f0 + v
    cn = [jnp.full((8, 128), -(R // 8.0), f32) for _ in cs]
    fi0 = d_ref[0:8, 128 * NT:128 * NT + 128]
    for r in range(8, R, 8):
        fi0 = fi0 + d_ref[r:r + 8, 128 * NT:128 * NT + 128]
    cm = [-fi0 for _ in cs]
    for r in range(0, R, 8):
        fi = d_ref[r:r + 8, 128 * NT:128 * NT + 128]
        an = jnp.full((8, 128), -float(NT), f32)
        am = -f0
        for t in range(NT):
            d = d_ref[r:r + 8, 128 * t:128 * t + 128]
            q = jnp.maximum(lax.rsqrt(jnp.maximum(d, 0.01)), 1.0)
            an = an + q
            am = am + q * fj[t]
            if t:
                cn[t] = cn[t] + q
                cm[t] = cm[t] + q * fi
        an_ref[r:r + 8, :] = an
        as_ref[r:r + 8, :] = am
        for part in parts[min(FR * r * len(parts) // R // 4, len(parts)):min(FR * (r + 8) * len(parts) // R // 4, len(parts))]:
            part()
    rows = [pl.ds(pl.multiple_of(c * 8, 8), 8) for c in cs]
    olds = [(jn_ref[rows[t], :], js_ref[rows[t], :]) for t in range(1, NT)]
    for t in range(1, NT):
        jn_ref[rows[t], :] = olds[t - 1][0] + cn[t]
        js_ref[rows[t], :] = olds[t - 1][1] + cm[t]


def tree(v, lo, hi, run):
    if hi - lo == 1:
        run(lo)
        return
    mid = (lo + hi) // 2

    @pl.when(v < mid)
    def _():
        tree(v, lo, mid, run)

    @pl.when(v >= mid)
    def _():
        tree(v, mid, hi, run)


def kern(MODE, sc_ref, cnt_ref, cells, out_ref,
         a_ref, b_ref, f_ref, jn_ref, js_ref, stage, stage_a, d0, d1, an0, as0, an1, as1):
    x0 = sc_ref[0]
    y0 = sc_ref[1]
    ra = lax.broadcasted_iota(jnp.int32, stage_a.shape, 0) % 64
    stage_a[...] = jnp.where((ra >= 8) & (ra < 11), 1.0, 0.0)
    rb = lax.broadcasted_iota(jnp.int32, stage.shape, 0) % 32
    stage[...] = jnp.where((rb >= 20) & (rb < 23), 1.0, 0.0)
    ri = lax.broadcasted_iota(jnp.int32, (32, 128), 0)
    rim = (jnp.where(ri == 8, SENT * SENT, 0.0) + jnp.where((ri >= 20) & (ri < 23), 1.0, 0.0)).astype(bf16)

    @pl.loop(0, 12)
    def _(col):
        for zz in (0, ZP - 1):
            b_ref[pl.ds(pl.multiple_of((col * ZP + zz) * 32, 32), 32), :] = rim
            f_ref[pl.ds(col * ZP + zz, 1), :] = jnp.zeros((1, 128), f32)

    @pl.loop(0, 12)
    def _(k):
        rows = pl.ds(pl.multiple_of(k * 8 * ZP, 8), 8 * ZP)
        jn_ref[rows, :] = jnp.zeros((8 * ZP, 128), f32)
        js_ref[rows, :] = jnp.zeros((8 * ZP, 128), f32)

    b = functools.partial(build_cols, x0=x0, y0=y0, b_ref=b_ref, f_ref=f_ref, a_ref=a_ref, stage=stage, stage_a=stage_a)

    @pl.loop(0, 4)
    def _(k):
        b(cells, k * 64, (k // 2) * 4 + k % 2 + 1, own_cell=k * 64)

    @pl.loop(0, 7)
    def _(k):
        col = jnp.where(k < 2, 3 + 4 * k, jnp.where(k < 3, 4, jnp.where(k < 6, 6 + k, 8)))
        b(cells, 256 + k * 64, col, own_cell=None)

    if MODE == "build":
        out_ref[...] = jnp.zeros_like(out_ref)
        return
    for part in make_d(0, d0, a_ref, b_ref):
        part()
    bufs = ((d0, an0, as0), (d1, an1, as1))

    @pl.loop(0, 128)
    def _(i):
        for p in range(2):
            cell = i * 2 + p
            nxt = jnp.minimum(cell + 1, 255)
            prev = jnp.maximum(cell - 1, 0)
            d, an, am = bufs[p]
            dn, anp, amp = bufs[1 - p]

            def run(k):
                parts = make_d(nxt, dn, a_ref, b_ref)
                finish(prev, anp, amp, out_ref)
                pair_sums(16 * k, cell, d, an, am, f_ref, jn_ref, js_ref, parts)
            tree((cnt_ref[cell] + 15) // 16, 0, 9, run)
    finish(255, an1, as1, out_ref)

    def side(col, z0, ref):
        base = (col * ZP + 1 + z0) * 8
        v = ref[pl.ds(base, 8, stride=8), :]
        for k in range(1, 8):
            v = v + ref[pl.ds(base + k, 8, stride=8), :]
        return v

    @pl.loop(0, 32)
    def _(k):
        cx, cy, z0 = k // 16, (k // 8) % 2, (k % 8) * 8
        rows = pl.ds(pl.multiple_of(k * 8, 8), 8)
        out_ref[0, rows, :] += side(cx * 4 + cy + 1, z0, jn_ref)
        out_ref[1, rows, :] += side(cx * 4 + cy + 1, z0, js_ref)

    @pl.loop(0, 8)
    def _(k):
        for h, col in enumerate((3, 7, 4, 9, 10, 11, 8)):
            rows = pl.ds(pl.multiple_of(256 + h * 64 + k * 8, 8), 8)
            out_ref[0, rows, :] = side(col, k * 8, jn_ref)
            out_ref[1, rows, :] = side(col, k * 8, js_ref)


def compute(sc, cnt, cells, MODE="full"):
    vm = pl.BlockSpec(memory_space=pltpu.VMEM)
    sm = pl.BlockSpec(memory_space=pltpu.SMEM)
    return pl.pallas_call(
        functools.partial(kern, MODE),
        out_shape=jax.ShapeDtypeStruct((2, 704, 128), f32),
        in_specs=[sm, sm, vm], out_specs=vm,
        scratch_shapes=[pltpu.VMEM((256 * 128, 64), bf16), pltpu.VMEM((12 * ZP * 32, 128), bf16),
                        pltpu.VMEM((12 * ZP, 128), f32), pltpu.VMEM((12 * ZP * 8, 128), f32), pltpu.VMEM((12 * ZP * 8, 128), f32),
                        pltpu.VMEM((256, 128), f32), pltpu.VMEM((512, 128), f32)]
        + [pltpu.VMEM((128, 128 * (NT + 1)), f32)] * 2 + [pltpu.VMEM((128, 128), f32)] * 4,
        compiler_params=pltpu.CompilerParams(vmem_limit_bytes=56 * 2**20),
        name="pairs",
    )(sc, cnt, cells)


def far(ds, dd):
    slab = lax.rem(lax.axis_index("slab") + (ds + N_SLAB), N_SLAB)
    dom = lax.rem(lax.axis_index("dom") + (dd + N_DOM), N_DOM)
    return (slab, dom)


def copy_to(src, dst, send, recv, where):
    return pltpu.make_async_remote_copy(
        src_ref=src, dst_ref=dst, send_sem=send, recv_sem=recv, device_id=far(*where),
        device_id_type=pl.DeviceIdType.MESH)


def greet(senders):
    barrier = pltpu.get_barrier_semaphore()
    for where in senders:
        pl.semaphore_signal(barrier, inc=1, device_id=far(*where), device_id_type=pl.DeviceIdType.MESH)
    pl.semaphore_wait(barrier, len(senders))


def picked(onehot, v, dims):
    out = None
    for part in reversed(split3(v)):
        p = lax.dot_general(onehot, part.astype(bf16), (dims, ((), ())), preferred_element_type=f32)
        out = p if out is None else out + p
    return out


def iota(shape, dim):
    return lax.broadcasted_iota(jnp.int32, shape, dim).astype(f32)


FAR = (0, 4, 1, 3)
HALO = ((0, 64, (-1, -1), 576), (64, 64, (-1, 1), 640), (0, 128, (-1, 0), 448), (0, 64, (0, -1), 256),
        (128, 64, (0, -1), 320), (192, 64, (0, 1), 384))


def relayout_kernel(x_ref, dest_ref, cnt_ref, cells, sent, got, parts, s1, r1, s2, r2):
    me = lax.axis_index("dom")
    greet([(0, -2), (0, -1), (0, 1), (0, 2), (1, 0), (1, 1), (1, -1)])
    dest = dest_ref[...]
    dom = lax.shift_right_logical(dest, 8)
    shift = (dom - me).astype(f32)
    shift = jnp.where(shift < -16.0, shift + 32.0, jnp.where(shift > 16.0, shift - 32.0, shift)) + 2.0
    local = (dest - dom * 256).astype(f32)
    chosen = jnp.where(iota((8, 256), 0) == shift, 1.0, 0.0)
    lower = jnp.where(iota((256, 256), 0) <= iota((256, 256), 1), 1.0, 0.0).astype(bf16)
    rank = jnp.dot(chosen.astype(bf16), lower, preferred_element_type=f32)
    rank = jnp.sum(chosen * rank, axis=0, keepdims=True) - 1.0
    slot = shift * 64.0 + rank
    xs = [x_ref[:, c, :] for c in range(4)]
    diag = jnp.where(iota((256, 256), 0) == iota((256, 256), 1), 1.0, 0.0)
    tag = jnp.broadcast_to(jnp.sum(diag * local, axis=1, keepdims=True) + 1.0, (256, 128))
    for c in range(4):
        for p, v in enumerate(split3(xs[c])):
            parts[p, :, 128 * c:128 * c + 128] = v.astype(bf16)
    tag = tag.astype(bf16)

    def send_part(k, dst):
        pack = jnp.where(iota((64, 256), 0) + 64.0 * k == slot, 1.0, 0.0).astype(bf16)
        out = [jnp.dot(pack, parts[p], preferred_element_type=f32) for p in (2, 1, 0)]
        dst[k, :, 0:512] = out[0] + out[1] + out[2]
        dst[k, :, 512:640] = jnp.dot(pack, tag, preferred_element_type=f32)
    first = []
    for k in FAR:
        send_part(k, sent)
        c = copy_to(sent.at[k], got.at[k], s1.at[k], r1.at[k], (0, k - 2))
        c.start()
        first.append(c)
    send_part(2, got)
    count = jnp.sum(diag * cnt_ref[...].astype(f32), axis=1, keepdims=True)
    filled = iota((256, 128), 1) < count
    for c in first:
        c.wait_recv()
    places = []
    for k in range(5):
        label = got[k, :, 512:640]
        lanes = iota((64, 128), 1)
        places.append(jnp.concatenate(
            [jnp.where(label == lanes + 1.0, 1.0, 0.0), jnp.where(label == lanes + 129.0, 1.0, 0.0)], 1))
    place = jnp.concatenate(places, 0).T.astype(bf16)
    total = picked(place, jnp.concatenate([got[k, :, 0:512] for k in range(5)], 0), ((1,), (0,)))
    x0 = (lax.axis_index("slab") * 2 + 1).astype(f32)
    cells[0:256, 0:128] = jnp.where(filled, total[:, 0:128], x0 + SENT)
    cells[0:256, 128:384] = total[:, 128:384]
    cells[0:256, 384:512] = jnp.where(filled, total[:, 384:512], 0.0)
    second = []
    for k, (row, rows, where, there) in enumerate(HALO):
        c = copy_to(cells.at[pl.ds(row, rows)], cells.at[pl.ds(there, rows)], s2.at[k], r2.at[k], where)
        c.start()
        second.append(c)
    for c in first:
        c.wait_send()
    for c in second:
        c.wait()


def relayout(x, dest, count):
    vm = pl.BlockSpec(memory_space=pltpu.VMEM)
    return pl.pallas_call(
        relayout_kernel,
        out_shape=jax.ShapeDtypeStruct((704, 512), f32),
        in_specs=[vm] * 3, out_specs=vm,
        scratch_shapes=[pltpu.VMEM((5, 64, 640), f32)] * 2 + [pltpu.VMEM((3, 256, 512), bf16)]
        + [pltpu.SemaphoreType.DMA((5,))] * 2 + [pltpu.SemaphoreType.DMA((6,))] * 2,
        compiler_params=pltpu.CompilerParams(collective_id=0, has_side_effects=True, vmem_limit_bytes=32 * 2**20),
        name="relayout",
    )(x, dest, count)


BACK = ((320, 64, (1, 1)), (384, 64, (1, -1)), (192, 128, (1, 0)), (0, 128, (0, 1)), (128, 64, (0, -1)))


def combine_kernel(sums, cells, cnt_ref, dens, lap, got, field, s1, r1, fsem):
    greet([(0, -1), (0, 1), (-1, 0), (-1, -1), (-1, 1)])
    fetch = pltpu.make_async_copy(cells.at[pl.ds(0, 256), pl.ds(384, 128)], field, fsem)
    fetch.start()
    copies = []
    for k, (row, rows, where) in enumerate(BACK):
        c = copy_to(sums.at[:, pl.ds(256 + row, rows)], got.at[:, pl.ds(row, rows)], s1.at[k], r1.at[k], where)
        c.start()
        copies.append(c)
    diag = jnp.where(iota((256, 256), 0) == iota((256, 256), 1), 1.0, 0.0)
    count = jnp.sum(diag * cnt_ref[...].astype(f32), axis=1, keepdims=True)
    fetch.wait()
    for c in copies:
        c.wait()
    own = lax.rsqrt(jnp.full((64, 128), 0.01, f32)) - 1.0
    lists = ((0, 192, 320), (256, 384), (64,), (128,))
    for q in range(4):
        rows = slice(64 * q, 64 * q + 64)
        n = sums[0, rows, :]
        s = sums[1, rows, :]
        for r in lists[q]:
            n = n + got[0, r:r + 64, :]
            s = s + got[1, r:r + 64, :]
        filled = iota((64, 128), 1) < count[rows]
        dens[rows, :] = jnp.where(filled, (n - own) / ref_density, 0.0)
        lap[rows, :] = jnp.where(filled, (s - field[rows, :] * n) / ref_density, 0.0)


def combine(sums, cells, count):
    vm = pl.BlockSpec(memory_space=pltpu.VMEM)
    return pl.pallas_call(
        combine_kernel,
        out_shape=[jax.ShapeDtypeStruct((256, 128), f32)] * 2,
        in_specs=[vm, pl.BlockSpec(memory_space=pl.ANY), vm], out_specs=[vm] * 2,
        scratch_shapes=[pltpu.VMEM((2, 448, 128), f32), pltpu.VMEM((256, 128), f32), pltpu.SemaphoreType.DMA((5,)), pltpu.SemaphoreType.DMA((5,)),
                        pltpu.SemaphoreType.DMA],
        compiler_params=pltpu.CompilerParams(collective_id=1, has_side_effects=True, vmem_limit_bytes=16 * 2**20),
        name="combine",
    )(sums, cells, count)


def local(incoming, dest, counts):
    count = counts.reshape(256)
    x0 = (lax.axis_index("slab") * 2 + 1).astype(f32)
    y0 = (lax.axis_index("dom") * 2 + 1).astype(f32)
    cells = relayout(incoming.reshape(256, 4, 128), dest, count.reshape(1, 256))
    sums = compute(jnp.stack([x0, y0]), count, cells)
    density, laplace = combine(sums, cells, count.reshape(1, 256))
    return density.reshape(2, 2, 64, 128), laplace.reshape(2, 2, 64, 128)


def solution(mesh):
    in_specs = (P("slab", "dom", None, None), P("slab", "dom"), P("slab", "dom", None))
    out_specs = (P("slab", "dom", None, None), P("slab", "dom", None, None))
    return jax.shard_map(local, mesh=mesh, in_specs=in_specs, out_specs=out_specs, check_vma=False)
```

```python
import functools
import jax, jax.numpy as jnp
from jax import lax
from jax.experimental import pallas as pl
from jax.experimental.pallas import tpu as pltpu
from jax.sharding import PartitionSpec as P

f32, bf16 = jnp.float32, jnp.bfloat16
SENT = 100.0
ZP = 66
ref_density = 268.0825731
N_SLAB, N_DOM = 4, 32

OFFS = [(0, 0, 0), (0, 0, 1)] + [(dx, dy, dz) for dx, dy in ((0, 1), (1, -1), (1, 0), (1, 1)) for dz in (-1, 0, 1)]
NT = len(OFFS)
FR = 5


def split3(v):
    h = v.astype(bf16).astype(f32)
    r = v - h
    m = r.astype(bf16).astype(f32)
    return h, m, r - m


def split2(v):
    h = v.astype(bf16).astype(f32)
    m = (v - h).astype(bf16).astype(f32)
    return h, m, h + m


def left(h, m):
    return [-2.0 * h, -2.0 * h, -2.0 * m, -2.0 * m]


def right(h, m):
    return [h, m, h, m]


def build_cols(p_ref, row0, col, x0, y0, own_cell, b_ref, f_ref, a_ref, stage, stage_a):
    @pl.loop(0, 8)
    def _(k):
        z0 = k * 8
        rows = pl.ds(pl.multiple_of(row0 + z0, 8), 8)
        zc = (lax.broadcasted_iota(jnp.int32, (8, 128), 0) + z0).astype(f32) + 0.5
        xh, xm, x = split2(p_ref[rows, 0:128] - x0)
        yh, ym, y = split2(p_ref[rows, 128:256] - y0)
        zh, zm, z = split2(p_ref[rows, 256:384] - zc)
        f = p_ref[rows, 384:512]
        f_ref[pl.ds(col * ZP + 1 + z0, 8), :] = f
        xy = x * x + y * y
        terms = dict(enumerate(right(xh, xm) + right(yh, ym) + list(split3(xy + z * z))))
        terms.update(enumerate(right(zh, zm), 16))
        for r, v in terms.items():
            stage[pl.ds(r, 8, stride=32), :] = v
        b_ref[pl.ds(pl.multiple_of((col * ZP + 1 + z0) * 32, 32), 256), :] = stage[...].astype(bf16)
        if own_cell is None:
            return
        terms = dict(enumerate(left(xh, xm) + left(yh, ym)))
        for k2, s in enumerate((-1.0, 0.0, 1.0)):
            h, m, zs = split2(z - s)
            terms.update(enumerate(left(h, m) + list(split3(xy + zs * zs)), 16 + 16 * k2))
        terms.update(enumerate(split3(f), 23))
        for r, v in terms.items():
            stage_a[pl.ds(r, 8, stride=64), :] = v
        for j in range(8):
            t = stage_a[j * 64:j * 64 + 64, :].T
            a_ref[pl.ds(pl.multiple_of((own_cell + z0 + j) * 128, 128), 128), :] = t.astype(bf16)


def cell_of(cell):
    cx, cy, z = cell // 128, (cell // 64) % 2, cell % 64
    return [((cx + dx) * 4 + cy + 1 + dy) * ZP + 1 + z + dz for dx, dy, dz in OFFS]


def make_d(cell, d_ref, a_ref, b_ref):
    a = a_ref[pl.ds(pl.multiple_of(cell * 128, 128), 128), :]
    zero = jnp.zeros((16, 128), bf16)
    ri = lax.broadcasted_iota(jnp.int32, (16, 128), 0)
    pick = jnp.where((ri >= 7) & (ri < 10), 1.0, 0.0).astype(bf16)
    ws = []
    for (dx, dy, dz), c in zip(OFFS, cell_of(cell)):
        b = b_ref[pl.ds(pl.multiple_of(c * 32, 32), 32), :]
        ws.append(jnp.concatenate([b[:16]] + [b[16:] if k == dz else zero for k in (-1, 0, 1)], 0))
    ws.append(jnp.concatenate([zero, pick, zero, zero], 0))

    def part(t, r):
        w = jnp.concatenate(ws[t:t + 2], 1)
        d_ref[r:r + 32, 128 * t:128 * t + w.shape[1]] = jnp.dot(a[r:r + 32], w, preferred_element_type=f32)
    return [functools.partial(part, t, r) for t in range(0, NT + 1, 2) for r in range(0, 128, 32)]


def finish(cell, an_ref, as_ref, out_ref):
    out_ref[0, pl.ds(cell, 1), :] = jnp.sum(an_ref[...].T, axis=0, keepdims=True)
    out_ref[1, pl.ds(cell, 1), :] = jnp.sum(as_ref[...].T, axis=0, keepdims=True)


def pair_sums(R, cell, d_ref, an_ref, as_ref, f_ref, jn_ref, js_ref, parts):
    if R == 0:
        for part in parts:
            part()
        return
    cs = cell_of(cell)
    fj = [jnp.broadcast_to(f_ref[pl.ds(c, 1), :], (8, 128)) for c in cs]
    f0 = fj[0]
    for v in fj[1:]:
        f0 = f0 + v
    cn = [jnp.full((8, 128), -(R // 8.0), f32) for _ in cs]
    fi0 = d_ref[0:8, 128 * NT:128 * NT + 128]
    for r in range(8, R, 8):
        fi0 = fi0 + d_ref[r:r + 8, 128 * NT:128 * NT + 128]
    cm = [-fi0 for _ in cs]
    for r in range(0, R, 8):
        fi = d_ref[r:r + 8, 128 * NT:128 * NT + 128]
        an = jnp.full((8, 128), -float(NT), f32)
        am = -f0
        for t in range(NT):
            d = d_ref[r:r + 8, 128 * t:128 * t + 128]
            q = jnp.maximum(lax.rsqrt(jnp.maximum(d, 0.01)), 1.0)
            an = an + q
            am = am + q * fj[t]
            if t:
                cn[t] = cn[t] + q
                cm[t] = cm[t] + q * fi
        an_ref[r:r + 8, :] = an
        as_ref[r:r + 8, :] = am
        for part in parts[min(FR * r * len(parts) // R // 4, len(parts)):min(FR * (r + 8) * len(parts) // R // 4, len(parts))]:
            part()
    rows = [pl.ds(pl.multiple_of(c * 8, 8), 8) for c in cs]
    olds = [(jn_ref[rows[t], :], js_ref[rows[t], :]) for t in range(1, NT)]
    for t in range(1, NT):
        jn_ref[rows[t], :] = olds[t - 1][0] + cn[t]
        js_ref[rows[t], :] = olds[t - 1][1] + cm[t]


def tree(v, lo, hi, run):
    if hi - lo == 1:
        run(lo)
        return
    mid = (lo + hi) // 2

    @pl.when(v < mid)
    def _():
        tree(v, lo, mid, run)

    @pl.when(v >= mid)
    def _():
        tree(v, mid, hi, run)


def centre():
    return (lax.axis_index("slab") * 2 + 1).astype(f32), (lax.axis_index("dom") * 2 + 1).astype(f32)


def kern(cnt_ref, cells, out_ref,
         a_ref, b_ref, f_ref, jn_ref, js_ref, stage, stage_a, d0, d1, an0, as0, an1, as1):
    x0, y0 = centre()
    ra = lax.broadcasted_iota(jnp.int32, stage_a.shape, 0) % 64
    stage_a[...] = jnp.where((ra >= 8) & (ra < 11), 1.0, 0.0)
    rb = lax.broadcasted_iota(jnp.int32, stage.shape, 0) % 32
    stage[...] = jnp.where((rb >= 20) & (rb < 23), 1.0, 0.0)
    ri = lax.broadcasted_iota(jnp.int32, (32, 128), 0)
    rim = (jnp.where(ri == 8, SENT * SENT, 0.0) + jnp.where((ri >= 20) & (ri < 23), 1.0, 0.0)).astype(bf16)

    @pl.loop(0, 12)
    def _(col):
        for zz in (0, ZP - 1):
            b_ref[pl.ds(pl.multiple_of((col * ZP + zz) * 32, 32), 32), :] = rim
            f_ref[pl.ds(col * ZP + zz, 1), :] = jnp.zeros((1, 128), f32)

    @pl.loop(0, 12)
    def _(k):
        rows = pl.ds(pl.multiple_of(k * 8 * ZP, 8), 8 * ZP)
        jn_ref[rows, :] = jnp.zeros((8 * ZP, 128), f32)
        js_ref[rows, :] = jnp.zeros((8 * ZP, 128), f32)

    b = functools.partial(build_cols, x0=x0, y0=y0, b_ref=b_ref, f_ref=f_ref, a_ref=a_ref, stage=stage, stage_a=stage_a)

    @pl.loop(0, 4)
    def _(k):
        b(cells, k * 64, (k // 2) * 4 + k % 2 + 1, own_cell=k * 64)

    @pl.loop(0, 7)
    def _(k):
        col = jnp.where(k < 2, 3 + 4 * k, jnp.where(k < 3, 4, jnp.where(k < 6, 6 + k, 8)))
        b(cells, 256 + k * 64, col, own_cell=None)

    for part in make_d(0, d0, a_ref, b_ref):
        part()
    bufs = ((d0, an0, as0), (d1, an1, as1))

    @pl.loop(0, 128)
    def _(i):
        for p in range(2):
            cell = i * 2 + p
            nxt = jnp.minimum(cell + 1, 255)
            prev = jnp.maximum(cell - 1, 0)
            d, an, am = bufs[p]
            dn, anp, amp = bufs[1 - p]

            def run(k):
                parts = make_d(nxt, dn, a_ref, b_ref)
                finish(prev, anp, amp, out_ref)
                pair_sums(16 * k, cell, d, an, am, f_ref, jn_ref, js_ref, parts)
            tree((cnt_ref[cell // 128, (cell // 64) % 2, cell % 64] + 15) // 16, 0, 9, run)
    finish(255, an1, as1, out_ref)

    def side(col, z0, ref):
        base = (col * ZP + 1 + z0) * 8
        v = ref[pl.ds(base, 8, stride=8), :]
        for k in range(1, 8):
            v = v + ref[pl.ds(base + k, 8, stride=8), :]
        return v

    @pl.loop(0, 32)
    def _(k):
        cx, cy, z0 = k // 16, (k // 8) % 2, (k % 8) * 8
        rows = pl.ds(pl.multiple_of(k * 8, 8), 8)
        out_ref[0, rows, :] += side(cx * 4 + cy + 1, z0, jn_ref)
        out_ref[1, rows, :] += side(cx * 4 + cy + 1, z0, js_ref)

    @pl.loop(0, 8)
    def _(k):
        for h, col in enumerate((3, 7, 4, 9, 10, 11, 8)):
            rows = pl.ds(pl.multiple_of(256 + h * 64 + k * 8, 8), 8)
            out_ref[0, rows, :] = side(col, k * 8, jn_ref)
            out_ref[1, rows, :] = side(col, k * 8, js_ref)


def compute(cnt, cells):
    vm = pl.BlockSpec(memory_space=pltpu.VMEM)
    sm = pl.BlockSpec(memory_space=pltpu.SMEM)
    return pl.pallas_call(
        kern,
        out_shape=jax.ShapeDtypeStruct((2, 704, 128), f32),
        in_specs=[sm, vm], out_specs=vm,
        scratch_shapes=[pltpu.VMEM((256 * 128, 64), bf16), pltpu.VMEM((12 * ZP * 32, 128), bf16),
                        pltpu.VMEM((12 * ZP, 128), f32), pltpu.VMEM((12 * ZP * 8, 128), f32), pltpu.VMEM((12 * ZP * 8, 128), f32),
                        pltpu.VMEM((256, 128), f32), pltpu.VMEM((512, 128), f32)]
        + [pltpu.VMEM((128, 128 * (NT + 1)), f32)] * 2 + [pltpu.VMEM((128, 128), f32)] * 4,
        compiler_params=pltpu.CompilerParams(vmem_limit_bytes=30 * 2**20),
        name="pairs",
    )(cnt, cells)


def far(ds, dd):
    slab = lax.rem(lax.axis_index("slab") + (ds + N_SLAB), N_SLAB)
    dom = lax.rem(lax.axis_index("dom") + (dd + N_DOM), N_DOM)
    return (slab, dom)


def copy_to(src, dst, send, recv, where):
    return pltpu.make_async_remote_copy(
        src_ref=src, dst_ref=dst, send_sem=send, recv_sem=recv, device_id=far(*where),
        device_id_type=pl.DeviceIdType.MESH)


def greet(senders):
    barrier = pltpu.get_barrier_semaphore()
    for where in senders:
        pl.semaphore_signal(barrier, inc=1, device_id=far(*where), device_id_type=pl.DeviceIdType.MESH)
    pl.semaphore_wait(barrier, len(senders))


def picked(onehot, v, dims):
    out = None
    for part in reversed(split3(v)):
        p = lax.dot_general(onehot, part.astype(bf16), (dims, ((), ())), preferred_element_type=f32)
        out = p if out is None else out + p
    return out


def iota(shape, dim):
    return lax.broadcasted_iota(jnp.int32, shape, dim).astype(f32)


FAR = (0, 4, 1, 3)
HALO = ((0, 64, (-1, 0), 448), (64, 64, (-1, 0), 512), (0, 64, (0, -1), 256), (128, 64, (0, -1), 320),
        (192, 64, (0, 1), 384), (448, 64, (0, -1), 576), (512, 64, (0, 1), 640))


def relayout_kernel(x_any, dest_ref, cnt_ref, cells, x_ref, sent, got, parts, s1, r1, s2, r2, xsem):
    fetch = pltpu.make_async_copy(x_any, x_ref, xsem)
    fetch.start()
    me = lax.axis_index("dom")
    greet([(0, -2), (0, -1), (0, 1), (0, 2), (1, 0)])
    dest = dest_ref[...]
    dom = lax.shift_right_logical(dest, 8)
    shift = (dom - me).astype(f32)
    shift = jnp.where(shift < -16.0, shift + 32.0, jnp.where(shift > 16.0, shift - 32.0, shift)) + 2.0
    local = (dest - dom * 256).astype(f32)
    chosen = jnp.where(iota((8, 256), 0) == shift, 1.0, 0.0)
    lower = jnp.where(iota((256, 256), 0) <= iota((256, 256), 1), 1.0, 0.0).astype(bf16)
    rank = jnp.dot(chosen.astype(bf16), lower, preferred_element_type=f32)
    rank = jnp.sum(chosen * rank, axis=0, keepdims=True) - 1.0
    slot = shift * 64.0 + rank
    tag = jnp.broadcast_to(local + 1.0, (8, 256)).astype(bf16)
    fetch.wait()
    for c in range(4):
        for p, v in enumerate(split3(x_ref[pl.ds(c, 256, stride=4), :])):
            parts[p, :, 128 * c:128 * c + 128] = v.astype(bf16)

    def send_part(k, dst):
        pack = jnp.where(iota((64, 256), 0) + 64.0 * k == slot, 1.0, 0.0).astype(bf16)
        out = [jnp.dot(pack, parts[p], preferred_element_type=f32) for p in (2, 1, 0)]
        dst[k, 0:64, :] = out[0] + out[1] + out[2]
        dst[k, 64:72, 0:64] = lax.dot_general(tag, pack, (((1,), (1,)), ((), ())), preferred_element_type=f32)
    sent[:, 64:72, :] = jnp.zeros((5, 8, 512), f32)
    first = []
    for k in FAR:
        send_part(k, sent)
        c = copy_to(sent.at[k], got.at[k], s1.at[k], r1.at[k], (0, k - 2))
        c.start()
        first.append(c)
    send_part(2, got)
    diag = jnp.where(iota((256, 256), 0) == iota((256, 256), 1), 1.0, 0.0)
    count = jnp.concatenate([cnt_ref[a, b:b + 1, :] for a in range(2) for b in range(2)], 1).astype(f32)
    count = jnp.sum(diag * count, axis=1, keepdims=True)
    filled = iota((256, 128), 1) < count
    for c in first:
        c.wait_recv()
    label = jnp.concatenate([got[k, 64:65, 0:64] for k in range(5)], 1)
    place = jnp.where(iota((256, 320), 0) + 1.0 == label, 1.0, 0.0).astype(bf16)
    total = picked(place, jnp.concatenate([got[k, 0:64, :] for k in range(5)], 0), ((1,), (0,)))
    x0, _ = centre()
    cells[0:256, 0:128] = jnp.where(filled, total[:, 0:128], x0 + SENT)
    cells[0:256, 128:384] = total[:, 128:384]
    cells[0:256, 384:512] = jnp.where(filled, total[:, 384:512], 0.0)
    second = []
    for k, (row, rows, where, there) in enumerate(HALO):
        if k >= 5:
            second[k - 5].wait_recv()
        c = copy_to(cells.at[pl.ds(row, rows)], cells.at[pl.ds(there, rows)], s2.at[k], r2.at[k], where)
        c.start()
        second.append(c)
    for c in first:
        c.wait_send()
    for k, c in enumerate(second):
        c.wait_send()
        if k >= 2:
            c.wait_recv()


def relayout(x, dest, count):
    vm = pl.BlockSpec(memory_space=pltpu.VMEM)
    return pl.pallas_call(
        relayout_kernel,
        out_shape=jax.ShapeDtypeStruct((704, 512), f32),
        in_specs=[pl.BlockSpec(memory_space=pl.ANY), vm, vm], out_specs=vm,
        scratch_shapes=[pltpu.VMEM((1024, 128), f32)] + [pltpu.VMEM((5, 72, 512), f32)] * 2
        + [pltpu.VMEM((3, 256, 512), bf16)]
        + [pltpu.SemaphoreType.DMA((5,))] * 2 + [pltpu.SemaphoreType.DMA((7,))] * 2 + [pltpu.SemaphoreType.DMA],
        compiler_params=pltpu.CompilerParams(collective_id=0, has_side_effects=True, vmem_limit_bytes=32 * 2**20),
        name="relayout",
    )(x, dest, count)


BACK = ((320, 64, (1, 1)), (384, 64, (1, -1)), (192, 128, (1, 0)), (0, 128, (0, 1)), (128, 64, (0, -1)))


def combine_kernel(sums, cells, dens, lap, got, own_cells, s1, r1, fsem):
    greet([(0, -1), (0, 1), (-1, 0), (-1, -1), (-1, 1)])
    fetch = pltpu.make_async_copy(cells.at[pl.ds(0, 256)], own_cells, fsem)
    fetch.start()
    copies = []
    for k, (row, rows, where) in enumerate(BACK):
        c = copy_to(sums.at[:, pl.ds(256 + row, rows)], got.at[:, pl.ds(row, rows)], s1.at[k], r1.at[k], where)
        c.start()
        copies.append(c)
    x0, _ = centre()
    fetch.wait()
    for c in copies:
        c.wait()
    own = lax.rsqrt(jnp.full((64, 128), 0.01, f32)) - 1.0
    lists = ((0, 192, 320), (256, 384), (64,), (128,))
    for q in range(4):
        rows = slice(64 * q, 64 * q + 64)
        n = sums[0, rows, :]
        s = sums[1, rows, :]
        for r in lists[q]:
            n = n + got[0, r:r + 64, :]
            s = s + got[1, r:r + 64, :]
        filled = own_cells[rows, 0:128] - x0 < 0.5 * SENT
        dens[rows, :] = jnp.where(filled, (n - own) / ref_density, 0.0)
        lap[rows, :] = jnp.where(filled, (s - own_cells[rows, 384:512] * n) / ref_density, 0.0)


def combine(sums, cells):
    vm = pl.BlockSpec(memory_space=pltpu.VMEM)
    return pl.pallas_call(
        combine_kernel,
        out_shape=[jax.ShapeDtypeStruct((256, 128), f32)] * 2,
        in_specs=[vm, pl.BlockSpec(memory_space=pl.ANY)], out_specs=[vm] * 2,
        scratch_shapes=[pltpu.VMEM((2, 448, 128), f32), pltpu.VMEM((256, 512), f32), pltpu.SemaphoreType.DMA((5,)), pltpu.SemaphoreType.DMA((5,)),
                        pltpu.SemaphoreType.DMA],
        compiler_params=pltpu.CompilerParams(collective_id=1, has_side_effects=True, vmem_limit_bytes=16 * 2**20),
        name="combine",
    )(sums, cells)


def local(incoming, dest, counts):
    cells = relayout(incoming.reshape(1024, 128), dest, counts)
    sums = compute(counts, cells)
    density, laplace = combine(sums, cells)
    return density.reshape(2, 2, 64, 128), laplace.reshape(2, 2, 64, 128)


def solution(mesh):
    in_specs = (P("slab", "dom", None, None), P("slab", "dom"), P("slab", "dom", None))
    out_specs = (P("slab", "dom", None, None), P("slab", "dom", None, None))
    return jax.shard_map(local, mesh=mesh, in_specs=in_specs, out_specs=out_specs, check_vma=False)
```

```python
import functools
import jax, jax.numpy as jnp
from jax import lax
from jax.experimental import pallas as pl
from jax.experimental.pallas import tpu as pltpu
from jax.sharding import PartitionSpec as P

f32, bf16 = jnp.float32, jnp.bfloat16
SENT = 100.0
ZP = 66
ref_density = 268.0825731
N_SLAB, N_DOM = 4, 32

OFFS = [(0, 0, 0), (0, 0, 1)] + [(dx, dy, dz) for dx, dy in ((0, 1), (1, -1), (1, 0), (1, 1)) for dz in (-1, 0, 1)]
NT = len(OFFS)
FR = 5


def split3(v):
    h = v.astype(bf16).astype(f32)
    r = v - h
    m = r.astype(bf16).astype(f32)
    return h, m, r - m


def split2(v):
    h = v.astype(bf16).astype(f32)
    m = (v - h).astype(bf16).astype(f32)
    return h, m, h + m


def left(h, m):
    return [-2.0 * h, -2.0 * h, -2.0 * m, -2.0 * m]


def right(h, m):
    return [h, m, h, m]


def build_cols(p_ref, row0, col, x0, y0, own_cell, b_ref, f_ref, stage, stage_a):
    @pl.loop(0, 8)
    def _(k):
        z0 = k * 8
        rows = pl.ds(pl.multiple_of(row0 + z0, 8), 8)
        zc = (lax.broadcasted_iota(jnp.int32, (8, 128), 0) + z0).astype(f32) + 0.5
        xh, xm, x = split2(p_ref[rows, 0:128] - x0)
        yh, ym, y = split2(p_ref[rows, 128:256] - y0)
        zh, zm, z = split2(p_ref[rows, 256:384] - zc)
        f = p_ref[rows, 384:512]
        f_ref[pl.ds(col * ZP + 1 + z0, 8), :] = f
        xy = x * x + y * y
        terms = dict(enumerate(right(xh, xm) + right(yh, ym) + list(split3(xy + z * z))))
        terms.update(enumerate(right(zh, zm), 16))
        for r, v in terms.items():
            stage[pl.ds(r, 8, stride=32), :] = v
        b_ref[pl.ds(pl.multiple_of((col * ZP + 1 + z0) * 32, 32), 256), :] = stage[...].astype(bf16)
        if own_cell is None:
            return
        terms = dict(enumerate(left(xh, xm) + left(yh, ym)))
        for k2, s in enumerate((-1.0, 0.0, 1.0)):
            h, m, zs = split2(z - s)
            terms.update(enumerate(left(h, m) + list(split3(xy + zs * zs)), 16 + 16 * k2))
        terms.update(enumerate(split3(f), 23))
        for r, v in terms.items():
            stage_a[pl.ds((own_cell + z0) * 64 + r, 8, stride=64), :] = v


def cell_of(cell):
    cell = jnp.asarray(cell, jnp.int32)
    cx, cy, z = cell >> 7, (cell >> 6) & 1, cell & 63
    return (cx * 4 + cy + 1) * ZP + 1 + z


STEPS = [(dx * 4 + dy) * ZP + dz for dx, dy, dz in OFFS]


def rows_of(base, count):
    first = base * count
    return [pl.ds(pl.multiple_of(first + step * count, count), count) for step in STEPS]


def turn(cell, a_ref, stage_a):
    a_ref[...] = stage_a[pl.ds(pl.multiple_of(cell * 64, 64), 64), :].T.astype(bf16)


def make_d(cell, d_ref, a_ref, b_ref):
    a = a_ref[...]
    zero = jnp.zeros((16, 128), bf16)
    ri = lax.broadcasted_iota(jnp.int32, (16, 128), 0)
    pick = jnp.where((ri >= 7) & (ri < 10), 1.0, 0.0).astype(bf16)
    ws = []
    for (dx, dy, dz), rows in zip(OFFS, rows_of(cell_of(cell), 32)):
        b = b_ref[rows, :]
        ws.append(jnp.concatenate([b[:16]] + [b[16:] if k == dz else zero for k in (-1, 0, 1)], 0))
    ws.append(jnp.concatenate([zero, pick, zero, zero], 0))

    def part(t, r):
        w = jnp.concatenate(ws[t:t + 2], 1)
        d_ref[r:r + 32, 128 * t:128 * t + w.shape[1]] = jnp.dot(a[r:r + 32], w, preferred_element_type=f32)
    return [functools.partial(part, t, r) for t in range(0, NT + 1, 2) for r in range(0, 128, 32)]


def finish(cell, an_ref, as_ref, out_ref):
    out_ref[0, pl.ds(cell, 1), :] = jnp.sum(an_ref[...].T, axis=0, keepdims=True)
    out_ref[1, pl.ds(cell, 1), :] = jnp.sum(as_ref[...].T, axis=0, keepdims=True)


def pair_sums(R, cell, d_ref, an_ref, as_ref, f_ref, jn_ref, js_ref, parts):
    if R == 0:
        for part in parts:
            part()
        return
    base = cell_of(cell)
    fj = [jnp.broadcast_to(f_ref[pl.ds(base + step, 1), :], (8, 128)) for step in STEPS]
    f0 = fj[0]
    for v in fj[1:]:
        f0 = f0 + v
    cn = [jnp.full((8, 128), -(R // 8.0), f32) for _ in STEPS]
    fi0 = d_ref[0:8, 128 * NT:128 * NT + 128]
    for r in range(8, R, 8):
        fi0 = fi0 + d_ref[r:r + 8, 128 * NT:128 * NT + 128]
    cm = [-fi0 for _ in STEPS]
    for r in range(0, R, 8):
        fi = d_ref[r:r + 8, 128 * NT:128 * NT + 128]
        an = jnp.full((8, 128), -float(NT), f32)
        am = -f0
        for t in range(NT):
            d = d_ref[r:r + 8, 128 * t:128 * t + 128]
            q = jnp.maximum(lax.rsqrt(jnp.maximum(d, 0.01)), 1.0)
            an = an + q
            am = am + q * fj[t]
            if t:
                cn[t] = cn[t] + q
                cm[t] = cm[t] + q * fi
        an_ref[r:r + 8, :] = an
        as_ref[r:r + 8, :] = am
        for part in parts[min(FR * r * len(parts) // R // 4, len(parts)):min(FR * (r + 8) * len(parts) // R // 4, len(parts))]:
            part()
    rows = rows_of(base, 8)
    olds = [(jn_ref[rows[t], :], js_ref[rows[t], :]) for t in range(1, NT)]
    for t in range(1, NT):
        jn_ref[rows[t], :] = olds[t - 1][0] + cn[t]
        js_ref[rows[t], :] = olds[t - 1][1] + cm[t]


def tree(v, lo, hi, run):
    if hi - lo == 1:
        run(lo)
        return
    mid = (lo + hi) // 2

    @pl.when(v < mid)
    def _():
        tree(v, lo, mid, run)

    @pl.when(v >= mid)
    def _():
        tree(v, mid, hi, run)


def centre():
    return (lax.axis_index("slab") * 2 + 1).astype(f32), (lax.axis_index("dom") * 2 + 1).astype(f32)


def kern(cnt_ref, cells, out_ref,
         a0, a1, b_ref, f_ref, jn_ref, js_ref, stage, stage_a, d0, d1, an0, as0, an1, as1):
    x0, y0 = centre()
    ra = lax.broadcasted_iota(jnp.int32, (64, 128), 0)
    ones = jnp.where((ra >= 8) & (ra < 11), 1.0, 0.0)

    @pl.loop(0, 256)
    def _(k):
        stage_a[pl.ds(pl.multiple_of(k * 64, 64), 64), :] = ones
    rb = lax.broadcasted_iota(jnp.int32, stage.shape, 0) % 32
    stage[...] = jnp.where((rb >= 20) & (rb < 23), 1.0, 0.0)
    ri = lax.broadcasted_iota(jnp.int32, (32, 128), 0)
    rim = (jnp.where(ri == 8, SENT * SENT, 0.0) + jnp.where((ri >= 20) & (ri < 23), 1.0, 0.0)).astype(bf16)

    @pl.loop(0, 12)
    def _(col):
        for zz in (0, ZP - 1):
            b_ref[pl.ds(pl.multiple_of((col * ZP + zz) * 32, 32), 32), :] = rim
            f_ref[pl.ds(col * ZP + zz, 1), :] = jnp.zeros((1, 128), f32)

    @pl.loop(0, 12)
    def _(k):
        rows = pl.ds(pl.multiple_of(k * 8 * ZP, 8), 8 * ZP)
        jn_ref[rows, :] = jnp.zeros((8 * ZP, 128), f32)
        js_ref[rows, :] = jnp.zeros((8 * ZP, 128), f32)

    b = functools.partial(build_cols, x0=x0, y0=y0, b_ref=b_ref, f_ref=f_ref, stage=stage, stage_a=stage_a)

    @pl.loop(0, 4)
    def _(k):
        b(cells, k * 64, (k // 2) * 4 + k % 2 + 1, own_cell=k * 64)

    @pl.loop(0, 7)
    def _(k):
        col = jnp.where(k < 2, 3 + 4 * k, jnp.where(k < 3, 4, jnp.where(k < 6, 6 + k, 8)))
        b(cells, 256 + k * 64, col, own_cell=None)

    turn(0, a0, stage_a)
    turn(1, a1, stage_a)
    for part in make_d(0, d0, a0, b_ref):
        part()
    bufs = ((d0, an0, as0, a0), (d1, an1, as1, a1))

    @pl.loop(0, 128)
    def _(i):
        for p in range(2):
            cell = i * 2 + p
            nxt = jnp.minimum(cell + 1, 255)
            prev = jnp.maximum(cell - 1, 0)
            d, an, am, a = bufs[p]
            dn, anp, amp, a_next = bufs[1 - p]
            later = jnp.minimum(cell + 2, 255)

            def run(k):
                turn(later, a, stage_a)
                parts = make_d(nxt, dn, a_next, b_ref)
                finish(prev, anp, amp, out_ref)
                pair_sums(16 * k, cell, d, an, am, f_ref, jn_ref, js_ref, parts)
            tree((cnt_ref[cell >> 7, (cell >> 6) & 1, cell & 63] + 15) >> 4, 0, 9, run)
    finish(255, an1, as1, out_ref)

    def side(col, z0, ref):
        base = (col * ZP + 1 + z0) * 8
        v = ref[pl.ds(base, 8, stride=8), :]
        for k in range(1, 8):
            v = v + ref[pl.ds(base + k, 8, stride=8), :]
        return v

    @pl.loop(0, 32)
    def _(k):
        cx, cy, z0 = k // 16, (k // 8) % 2, (k % 8) * 8
        rows = pl.ds(pl.multiple_of(k * 8, 8), 8)
        out_ref[0, rows, :] += side(cx * 4 + cy + 1, z0, jn_ref)
        out_ref[1, rows, :] += side(cx * 4 + cy + 1, z0, js_ref)

    @pl.loop(0, 8)
    def _(k):
        for h, col in enumerate((3, 7, 4, 9, 10, 11, 8)):
            rows = pl.ds(pl.multiple_of(256 + h * 64 + k * 8, 8), 8)
            out_ref[0, rows, :] = side(col, k * 8, jn_ref)
            out_ref[1, rows, :] = side(col, k * 8, js_ref)


def compute(cnt, cells):
    vm = pl.BlockSpec(memory_space=pltpu.VMEM)
    sm = pl.BlockSpec(memory_space=pltpu.SMEM)
    return pl.pallas_call(
        kern,
        out_shape=jax.ShapeDtypeStruct((2, 704, 128), f32),
        in_specs=[sm, vm], out_specs=vm,
        scratch_shapes=[pltpu.VMEM((128, 64), bf16), pltpu.VMEM((128, 64), bf16), pltpu.VMEM((12 * ZP * 32, 128), bf16),
                        pltpu.VMEM((12 * ZP, 128), f32), pltpu.VMEM((12 * ZP * 8, 128), f32), pltpu.VMEM((12 * ZP * 8, 128), f32),
                        pltpu.VMEM((256, 128), f32), pltpu.VMEM((256 * 64, 128), f32)]
        + [pltpu.VMEM((128, 128 * (NT + 1)), f32)] * 2 + [pltpu.VMEM((128, 128), f32)] * 4,
        compiler_params=pltpu.CompilerParams(vmem_limit_bytes=30 * 2**20),
        name="pairs",
    )(cnt, cells)


def far(ds, dd):
    slab = lax.rem(lax.axis_index("slab") + (ds + N_SLAB), N_SLAB)
    dom = lax.rem(lax.axis_index("dom") + (dd + N_DOM), N_DOM)
    return (slab, dom)


def copy_to(src, dst, send, recv, where):
    return pltpu.make_async_remote_copy(
        src_ref=src, dst_ref=dst, send_sem=send, recv_sem=recv, device_id=far(*where),
        device_id_type=pl.DeviceIdType.MESH)


def greet(senders):
    barrier = pltpu.get_barrier_semaphore()
    for where in senders:
        pl.semaphore_signal(barrier, inc=1, device_id=far(*where), device_id_type=pl.DeviceIdType.MESH)
    pl.semaphore_wait(barrier, len(senders))


def picked(onehot, v, dims):
    out = None
    for part in reversed(split3(v)):
        p = lax.dot_general(onehot, part.astype(bf16), (dims, ((), ())), preferred_element_type=f32)
        out = p if out is None else out + p
    return out


def iota(shape, dim):
    return lax.broadcasted_iota(jnp.int32, shape, dim).astype(f32)


FAR = (0, 4, 1, 3)
HALO = ((0, 64, (-1, 0), 448), (64, 64, (-1, 0), 512), (0, 64, (0, -1), 256), (128, 64, (0, -1), 320),
        (192, 64, (0, 1), 384), (448, 64, (0, -1), 576), (512, 64, (0, 1), 640))


def relayout_kernel(x_any, dest_ref, cnt_ref, cells, x_ref, sent, got, parts, s1, r1, s2, r2, xsem):
    fetch = pltpu.make_async_copy(x_any, x_ref, xsem)
    fetch.start()
    me = lax.axis_index("dom")
    greet([(0, -2), (0, -1), (0, 1), (0, 2), (1, 0)])
    dest = dest_ref[...]
    dom = lax.shift_right_logical(dest, 8)
    shift = (dom - me).astype(f32)
    shift = jnp.where(shift < -16.0, shift + 32.0, jnp.where(shift > 16.0, shift - 32.0, shift)) + 2.0
    local = (dest - dom * 256).astype(f32)
    chosen = jnp.where(iota((8, 256), 0) == shift, 1.0, 0.0)
    lower = jnp.where(iota((256, 256), 0) <= iota((256, 256), 1), 1.0, 0.0).astype(bf16)
    rank = jnp.dot(chosen.astype(bf16), lower, preferred_element_type=f32)
    rank = jnp.sum(chosen * rank, axis=0, keepdims=True) - 1.0
    slot = shift * 64.0 + rank
    tag = jnp.broadcast_to(local + 1.0, (8, 256)).astype(bf16)
    fetch.wait()
    for c in range(4):
        for p, v in enumerate(split3(x_ref[pl.ds(c, 256, stride=4), :])):
            parts[p, :, 128 * c:128 * c + 128] = v.astype(bf16)

    def send_part(k, dst):
        pack = jnp.where(iota((64, 256), 0) + 64.0 * k == slot, 1.0, 0.0).astype(bf16)
        out = [jnp.dot(pack, parts[p], preferred_element_type=f32) for p in (2, 1, 0)]
        dst[k, 0:64, :] = out[0] + out[1] + out[2]
        dst[k, 64:72, 0:64] = lax.dot_general(tag, pack, (((1,), (1,)), ((), ())), preferred_element_type=f32)
    sent[:, 64:72, :] = jnp.zeros((5, 8, 512), f32)
    first = []
    for k in FAR:
        send_part(k, sent)
        c = copy_to(sent.at[k], got.at[k], s1.at[k], r1.at[k], (0, k - 2))
        c.start()
        first.append(c)
    send_part(2, got)
    diag = jnp.where(iota((256, 256), 0) == iota((256, 256), 1), 1.0, 0.0)
    count = jnp.concatenate([cnt_ref[a, b:b + 1, :] for a in range(2) for b in range(2)], 1).astype(f32)
    count = jnp.sum(diag * count, axis=1, keepdims=True)
    filled = iota((256, 128), 1) < count
    for c in first:
        c.wait_recv()
    label = jnp.concatenate([got[k, 64:65, 0:64] for k in range(5)], 1)
    place = jnp.where(iota((256, 320), 0) + 1.0 == label, 1.0, 0.0).astype(bf16)
    total = picked(place, jnp.concatenate([got[k, 0:64, :] for k in range(5)], 0), ((1,), (0,)))
    x0, _ = centre()
    cells[0:256, 0:128] = jnp.where(filled, total[:, 0:128], x0 + SENT)
    cells[0:256, 128:384] = total[:, 128:384]
    cells[0:256, 384:512] = jnp.where(filled, total[:, 384:512], 0.0)
    second = []
    for k, (row, rows, where, there) in enumerate(HALO):
        if k >= 5:
            second[k - 5].wait_recv()
        c = copy_to(cells.at[pl.ds(row, rows)], cells.at[pl.ds(there, rows)], s2.at[k], r2.at[k], where)
        c.start()
        second.append(c)
    for c in first:
        c.wait_send()
    for k, c in enumerate(second):
        c.wait_send()
        if k >= 2:
            c.wait_recv()


def relayout(x, dest, count):
    vm = pl.BlockSpec(memory_space=pltpu.VMEM)
    return pl.pallas_call(
        relayout_kernel,
        out_shape=jax.ShapeDtypeStruct((704, 512), f32),
        in_specs=[pl.BlockSpec(memory_space=pl.ANY), vm, vm], out_specs=vm,
        scratch_shapes=[pltpu.VMEM((1024, 128), f32)] + [pltpu.VMEM((5, 72, 512), f32)] * 2
        + [pltpu.VMEM((3, 256, 512), bf16)]
        + [pltpu.SemaphoreType.DMA((5,))] * 2 + [pltpu.SemaphoreType.DMA((7,))] * 2 + [pltpu.SemaphoreType.DMA],
        compiler_params=pltpu.CompilerParams(collective_id=0, has_side_effects=True, vmem_limit_bytes=32 * 2**20),
        name="relayout",
    )(x, dest, count)


BACK = ((320, 64, (1, 1)), (384, 64, (1, -1)), (192, 128, (1, 0)), (0, 128, (0, 1)), (128, 64, (0, -1)))


def combine_kernel(sums, cells, dens, lap, got, own_cells, s1, r1, fsem):
    greet([(0, -1), (0, 1), (-1, 0), (-1, -1), (-1, 1)])
    fetch = pltpu.make_async_copy(cells.at[pl.ds(0, 256)], own_cells, fsem)
    fetch.start()
    copies = []
    for k, (row, rows, where) in enumerate(BACK):
        c = copy_to(sums.at[:, pl.ds(256 + row, rows)], got.at[:, pl.ds(row, rows)], s1.at[k], r1.at[k], where)
        c.start()
        copies.append(c)
    x0, _ = centre()
    fetch.wait()
    for c in copies:
        c.wait()
    own = lax.rsqrt(jnp.full((64, 128), 0.01, f32)) - 1.0
    lists = ((0, 192, 320), (256, 384), (64,), (128,))
    for q in range(4):
        rows = slice(64 * q, 64 * q + 64)
        n = sums[0, rows, :]
        s = sums[1, rows, :]
        for r in lists[q]:
            n = n + got[0, r:r + 64, :]
            s = s + got[1, r:r + 64, :]
        filled = own_cells[rows, 0:128] - x0 < 0.5 * SENT
        dens[rows, :] = jnp.where(filled, (n - own) / ref_density, 0.0)
        lap[rows, :] = jnp.where(filled, (s - own_cells[rows, 384:512] * n) / ref_density, 0.0)


def combine(sums, cells):
    vm = pl.BlockSpec(memory_space=pltpu.VMEM)
    return pl.pallas_call(
        combine_kernel,
        out_shape=[jax.ShapeDtypeStruct((256, 128), f32)] * 2,
        in_specs=[vm, pl.BlockSpec(memory_space=pl.ANY)], out_specs=[vm] * 2,
        scratch_shapes=[pltpu.VMEM((2, 448, 128), f32), pltpu.VMEM((256, 512), f32), pltpu.SemaphoreType.DMA((5,)), pltpu.SemaphoreType.DMA((5,)),
                        pltpu.SemaphoreType.DMA],
        compiler_params=pltpu.CompilerParams(collective_id=1, has_side_effects=True, vmem_limit_bytes=16 * 2**20),
        name="combine",
    )(sums, cells)


def local(incoming, dest, counts):
    cells = relayout(incoming.reshape(1024, 128), dest, counts)
    sums = compute(counts, cells)
    density, laplace = combine(sums, cells)
    return density.reshape(2, 2, 64, 128), laplace.reshape(2, 2, 64, 128)


def solution(mesh):
    in_specs = (P("slab", "dom", None, None), P("slab", "dom"), P("slab", "dom", None))
    out_specs = (P("slab", "dom", None, None), P("slab", "dom", None, None))
    return jax.shard_map(local, mesh=mesh, in_specs=in_specs, out_specs=out_specs, check_vma=False)
```

```python
import functools
import jax, jax.numpy as jnp
from jax import lax
from jax.experimental import pallas as pl
from jax.experimental.pallas import tpu as pltpu
from jax.sharding import PartitionSpec as P

f32, bf16 = jnp.float32, jnp.bfloat16
SENT = 100.0
ZP = 66
ref_density = 268.0825731
N_SLAB, N_DOM = 4, 32

OFFS = [(0, 0, 0), (0, 0, 1)] + [(dx, dy, dz) for dx, dy in ((0, 1), (1, -1), (1, 0), (1, 1)) for dz in (-1, 0, 1)]
NT = len(OFFS)
FR = 5


def split3(v):
    h = v.astype(bf16).astype(f32)
    r = v - h
    m = r.astype(bf16).astype(f32)
    return h, m, r - m


def split2(v):
    h = v.astype(bf16).astype(f32)
    m = (v - h).astype(bf16).astype(f32)
    return h, m, h + m


def left(h, m):
    return [-2.0 * h, -2.0 * h, -2.0 * m, -2.0 * m]


def right(h, m):
    return [h, m, h, m]


def build_cols(p_ref, row0, col, x0, y0, own_cell, b_ref, f_ref, stage, stage_a):
    @pl.loop(0, 8)
    def _(k):
        z0 = k * 8
        rows = pl.ds(pl.multiple_of(row0 + z0, 8), 8)
        zc = (lax.broadcasted_iota(jnp.int32, (8, 128), 0) + z0).astype(f32) + 0.5
        xh, xm, x = split2(p_ref[rows, 0:128] - x0)
        yh, ym, y = split2(p_ref[rows, 128:256] - y0)
        zh, zm, z = split2(p_ref[rows, 256:384] - zc)
        f = p_ref[rows, 384:512]
        f_ref[pl.ds(col * ZP + 1 + z0, 8), :] = f
        xy = x * x + y * y
        terms = dict(enumerate(right(xh, xm) + right(yh, ym) + list(split3(xy + z * z))))
        terms.update(enumerate(right(zh, zm), 16))
        for r, v in terms.items():
            stage[pl.ds(r, 8, stride=32), :] = v
        b_ref[pl.ds(pl.multiple_of((col * ZP + 1 + z0) * 32, 32), 256), :] = stage[...].astype(bf16)
        if own_cell is None:
            return
        terms = dict(enumerate(left(xh, xm) + left(yh, ym)))
        for k2, s in enumerate((-1.0, 0.0, 1.0)):
            h, m, zs = split2(z - s)
            terms.update(enumerate(left(h, m) + list(split3(xy + zs * zs)), 16 + 16 * k2))
        terms.update(enumerate(split3(f), 23))
        for r, v in terms.items():
            stage_a[pl.ds((own_cell + z0) * 64 + r, 8, stride=64), :] = v


def cell_of(cell):
    cell = jnp.asarray(cell, jnp.int32)
    cx, cy, z = cell >> 7, (cell >> 6) & 1, cell & 63
    return (cx * 4 + cy + 1) * ZP + 1 + z


STEPS = [(dx * 4 + dy) * ZP + dz for dx, dy, dz in OFFS]


def rows_of(base, count):
    first = base * count
    return [pl.ds(pl.multiple_of(first + step * count, count), count) for step in STEPS]


def turn(cell, a_ref, stage_a):
    a_ref[...] = stage_a[pl.ds(pl.multiple_of(cell * 64, 64), 64), :].T.astype(bf16)


def make_d(cell, d_ref, a_ref, b_ref):
    a = a_ref[...]
    zero = jnp.zeros((16, 128), bf16)
    ri = lax.broadcasted_iota(jnp.int32, (16, 128), 0)
    pick = jnp.where((ri >= 7) & (ri < 10), 1.0, 0.0).astype(bf16)
    ws = []
    for (dx, dy, dz), rows in zip(OFFS, rows_of(cell_of(cell), 32)):
        b = b_ref[rows, :]
        ws.append(jnp.concatenate([b[:16]] + [b[16:] if k == dz else zero for k in (-1, 0, 1)], 0))
    ws.append(jnp.concatenate([zero, pick, zero, zero], 0))

    def part(t, r):
        w = jnp.concatenate(ws[t:t + 2], 1)
        d_ref[r:r + 32, 128 * t:128 * t + w.shape[1]] = jnp.dot(a[r:r + 32], w, preferred_element_type=f32)
    return [functools.partial(part, t, r) for t in range(0, NT + 1, 2) for r in range(0, 128, 32)]


def finish(cell, an_ref, as_ref, out_ref):
    out_ref[0, pl.ds(cell, 1), :] = jnp.sum(an_ref[...].T, axis=0, keepdims=True)
    out_ref[1, pl.ds(cell, 1), :] = jnp.sum(as_ref[...].T, axis=0, keepdims=True)


def pair_sums(R, cell, d_ref, an_ref, as_ref, f_ref, jn_ref, js_ref, parts):
    if R == 0:
        for part in parts:
            part()
        return
    base = cell_of(cell)
    fj = [jnp.broadcast_to(f_ref[pl.ds(base + step, 1), :], (8, 128)) for step in STEPS]
    f0 = fj[0]
    for v in fj[1:]:
        f0 = f0 + v
    cn = [jnp.full((8, 128), -(R // 8.0), f32) for _ in STEPS]
    fi0 = d_ref[0:8, 128 * NT:128 * NT + 128]
    for r in range(8, R, 8):
        fi0 = fi0 + d_ref[r:r + 8, 128 * NT:128 * NT + 128]
    cm = [-fi0 for _ in STEPS]
    for r in range(0, R, 8):
        fi = d_ref[r:r + 8, 128 * NT:128 * NT + 128]
        an = jnp.full((8, 128), -float(NT), f32)
        am = -f0
        for t in range(NT):
            d = d_ref[r:r + 8, 128 * t:128 * t + 128]
            q = jnp.maximum(lax.rsqrt(jnp.maximum(d, 0.01)), 1.0)
            an = an + q
            am = am + q * fj[t]
            if t:
                cn[t] = cn[t] + q
                cm[t] = cm[t] + q * fi
        an_ref[r:r + 8, :] = an
        as_ref[r:r + 8, :] = am
        for part in parts[min(FR * r * len(parts) // R // 4, len(parts)):min(FR * (r + 8) * len(parts) // R // 4, len(parts))]:
            part()
    rows = rows_of(base, 8)
    olds = [(jn_ref[rows[t], :], js_ref[rows[t], :]) for t in range(1, NT)]
    for t in range(1, NT):
        jn_ref[rows[t], :] = olds[t - 1][0] + cn[t]
        js_ref[rows[t], :] = olds[t - 1][1] + cm[t]


def tree(v, lo, hi, run):
    if hi - lo == 1:
        run(lo)
        return
    mid = (lo + hi) // 2

    @pl.when(v < mid)
    def _():
        tree(v, lo, mid, run)

    @pl.when(v >= mid)
    def _():
        tree(v, mid, hi, run)


def centre():
    return (lax.axis_index("slab") * 2 + 1).astype(f32), (lax.axis_index("dom") * 2 + 1).astype(f32)


def kern(cnt_ref, cells, out_ref,
         a0, a1, b_ref, f_ref, jn_ref, js_ref, stage, stage_a, d0, d1, an0, as0, an1, as1):
    x0, y0 = centre()
    ra = lax.broadcasted_iota(jnp.int32, (64, 128), 0)
    ones = jnp.where((ra >= 8) & (ra < 11), 1.0, 0.0)

    @pl.loop(0, 32)
    def _(k):
        for j in range(8):
            stage_a[pl.ds(pl.multiple_of(k * 512 + 64 * j, 64), 64), :] = ones
    rb = lax.broadcasted_iota(jnp.int32, stage.shape, 0) % 32
    stage[...] = jnp.where((rb >= 20) & (rb < 23), 1.0, 0.0)
    ri = lax.broadcasted_iota(jnp.int32, (32, 128), 0)
    rim = (jnp.where(ri == 8, SENT * SENT, 0.0) + jnp.where((ri >= 20) & (ri < 23), 1.0, 0.0)).astype(bf16)

    @pl.loop(0, 12)
    def _(col):
        for zz in (0, ZP - 1):
            b_ref[pl.ds(pl.multiple_of((col * ZP + zz) * 32, 32), 32), :] = rim
            f_ref[pl.ds(col * ZP + zz, 1), :] = jnp.zeros((1, 128), f32)

    @pl.loop(0, 12)
    def _(k):
        rows = pl.ds(pl.multiple_of(k * 8 * ZP, 8), 8 * ZP)
        jn_ref[rows, :] = jnp.zeros((8 * ZP, 128), f32)
        js_ref[rows, :] = jnp.zeros((8 * ZP, 128), f32)

    b = functools.partial(build_cols, x0=x0, y0=y0, b_ref=b_ref, f_ref=f_ref, stage=stage, stage_a=stage_a)

    @pl.loop(0, 4)
    def _(k):
        b(cells, k * 64, (k // 2) * 4 + k % 2 + 1, own_cell=k * 64)

    @pl.loop(0, 7)
    def _(k):
        col = jnp.where(k < 2, 3 + 4 * k, jnp.where(k < 3, 4, jnp.where(k < 6, 6 + k, 8)))
        b(cells, 256 + k * 64, col, own_cell=None)

    turn(0, a0, stage_a)
    turn(1, a1, stage_a)
    for part in make_d(0, d0, a0, b_ref):
        part()
    bufs = ((d0, an0, as0, a0), (d1, an1, as1, a1))

    @pl.loop(0, 128)
    def _(i):
        for p in range(2):
            cell = i * 2 + p
            nxt = jnp.minimum(cell + 1, 255)
            prev = jnp.maximum(cell - 1, 0)
            d, an, am, a = bufs[p]
            dn, anp, amp, a_next = bufs[1 - p]
            later = jnp.minimum(cell + 2, 255)

            def run(k):
                turn(later, a, stage_a)
                parts = make_d(nxt, dn, a_next, b_ref)
                finish(prev, anp, amp, out_ref)
                pair_sums(16 * k, cell, d, an, am, f_ref, jn_ref, js_ref, parts)
            tree((cnt_ref[cell >> 7, (cell >> 6) & 1, cell & 63] + 15) >> 4, 0, 9, run)
    finish(255, an1, as1, out_ref)

    def side(col, z0, ref):
        base = (col * ZP + 1 + z0) * 8
        v = ref[pl.ds(base, 8, stride=8), :]
        for k in range(1, 8):
            v = v + ref[pl.ds(base + k, 8, stride=8), :]
        return v

    @pl.loop(0, 32)
    def _(k):
        cx, cy, z0 = k // 16, (k // 8) % 2, (k % 8) * 8
        rows = pl.ds(pl.multiple_of(k * 8, 8), 8)
        out_ref[0, rows, :] += side(cx * 4 + cy + 1, z0, jn_ref)
        out_ref[1, rows, :] += side(cx * 4 + cy + 1, z0, js_ref)

    @pl.loop(0, 8)
    def _(k):
        for h, col in enumerate((3, 7, 4, 9, 10, 11, 8)):
            rows = pl.ds(pl.multiple_of(256 + h * 64 + k * 8, 8), 8)
            out_ref[0, rows, :] = side(col, k * 8, jn_ref)
            out_ref[1, rows, :] = side(col, k * 8, js_ref)


def compute(cnt, cells):
    vm = pl.BlockSpec(memory_space=pltpu.VMEM)
    sm = pl.BlockSpec(memory_space=pltpu.SMEM)
    return pl.pallas_call(
        kern,
        out_shape=jax.ShapeDtypeStruct((2, 704, 128), f32),
        in_specs=[sm, vm], out_specs=vm,
        scratch_shapes=[pltpu.VMEM((128, 64), bf16), pltpu.VMEM((128, 64), bf16), pltpu.VMEM((12 * ZP * 32, 128), bf16),
                        pltpu.VMEM((12 * ZP, 128), f32), pltpu.VMEM((12 * ZP * 8, 128), f32), pltpu.VMEM((12 * ZP * 8, 128), f32),
                        pltpu.VMEM((256, 128), f32), pltpu.VMEM((256 * 64, 128), f32)]
        + [pltpu.VMEM((128, 128 * (NT + 1)), f32)] * 2 + [pltpu.VMEM((128, 128), f32)] * 4,
        compiler_params=pltpu.CompilerParams(vmem_limit_bytes=30 * 2**20),
        name="pairs",
    )(cnt, cells)


def far(ds, dd):
    slab = lax.rem(lax.axis_index("slab") + (ds + N_SLAB), N_SLAB)
    dom = lax.rem(lax.axis_index("dom") + (dd + N_DOM), N_DOM)
    return (slab, dom)


def copy_to(src, dst, send, recv, where):
    return pltpu.make_async_remote_copy(
        src_ref=src, dst_ref=dst, send_sem=send, recv_sem=recv, device_id=far(*where),
        device_id_type=pl.DeviceIdType.MESH)


def greet(senders):
    barrier = pltpu.get_barrier_semaphore()
    for where in senders:
        pl.semaphore_signal(barrier, inc=1, device_id=far(*where), device_id_type=pl.DeviceIdType.MESH)
    pl.semaphore_wait(barrier, len(senders))


def picked(onehot, v, dims):
    out = None
    for part in reversed(split3(v)):
        p = lax.dot_general(onehot, part.astype(bf16), (dims, ((), ())), preferred_element_type=f32)
        out = p if out is None else out + p
    return out


def iota(shape, dim):
    return lax.broadcasted_iota(jnp.int32, shape, dim).astype(f32)


FAR = (0, 4, 1, 3)
HALO = ((0, 64, (-1, 0), 448), (64, 64, (-1, 0), 512), (0, 64, (0, -1), 256), (128, 64, (0, -1), 320),
        (192, 64, (0, 1), 384), (448, 64, (0, -1), 576), (512, 64, (0, 1), 640))


def relayout_kernel(x_any, dest_ref, cnt_ref, cells, x_ref, sent, got, parts, s1, r1, s2, r2, xsem):
    fetch = pltpu.make_async_copy(x_any, x_ref, xsem)
    fetch.start()
    me = lax.axis_index("dom")
    greet([(0, -2), (0, -1), (0, 1), (0, 2), (1, 0)])
    dest = dest_ref[...]
    dom = lax.shift_right_logical(dest, 8)
    shift = (dom - me).astype(f32)
    shift = jnp.where(shift < -16.0, shift + 32.0, jnp.where(shift > 16.0, shift - 32.0, shift)) + 2.0
    local = (dest - dom * 256).astype(f32)
    chosen = jnp.where(iota((8, 256), 0) == shift, 1.0, 0.0)
    lower = jnp.where(iota((256, 256), 0) <= iota((256, 256), 1), 1.0, 0.0).astype(bf16)
    rank = jnp.dot(chosen.astype(bf16), lower, preferred_element_type=f32)
    rank = jnp.sum(chosen * rank, axis=0, keepdims=True) - 1.0
    slot = shift * 64.0 + rank
    tag = jnp.broadcast_to(local + 1.0, (8, 256)).astype(bf16)
    fetch.wait()
    for c in range(4):
        for p, v in enumerate(split3(x_ref[pl.ds(c, 256, stride=4), :])):
            parts[p, :, 128 * c:128 * c + 128] = v.astype(bf16)

    def send_part(k, dst):
        pack = jnp.where(iota((64, 256), 0) + 64.0 * k == slot, 1.0, 0.0).astype(bf16)
        out = [jnp.dot(pack, parts[p], preferred_element_type=f32) for p in (2, 1, 0)]
        dst[k, 0:64, :] = out[0] + out[1] + out[2]
        dst[k, 64:72, 0:64] = lax.dot_general(tag, pack, (((1,), (1,)), ((), ())), preferred_element_type=f32)
    sent[:, 64:72, :] = jnp.zeros((5, 8, 512), f32)
    first = []
    for k in FAR:
        send_part(k, sent)
        c = copy_to(sent.at[k], got.at[k], s1.at[k], r1.at[k], (0, k - 2))
        c.start()
        first.append(c)
    send_part(2, got)
    diag = jnp.where(iota((256, 256), 0) == iota((256, 256), 1), 1.0, 0.0)
    count = jnp.concatenate([cnt_ref[a, b:b + 1, :] for a in range(2) for b in range(2)], 1).astype(f32)
    count = jnp.sum(diag * count, axis=1, keepdims=True)
    filled = iota((256, 128), 1) < count
    for c in first:
        c.wait_recv()
    label = jnp.concatenate([got[k, 64:65, 0:64] for k in range(5)], 1)
    place = jnp.where(iota((256, 320), 0) + 1.0 == label, 1.0, 0.0).astype(bf16)
    total = picked(place, jnp.concatenate([got[k, 0:64, :] for k in range(5)], 0), ((1,), (0,)))
    x0, _ = centre()
    cells[0:256, 0:128] = jnp.where(filled, total[:, 0:128], x0 + SENT)
    cells[0:256, 128:384] = total[:, 128:384]
    cells[0:256, 384:512] = jnp.where(filled, total[:, 384:512], 0.0)
    second = []
    for k, (row, rows, where, there) in enumerate(HALO):
        if k >= 5:
            second[k - 5].wait_recv()
        c = copy_to(cells.at[pl.ds(row, rows)], cells.at[pl.ds(there, rows)], s2.at[k], r2.at[k], where)
        c.start()
        second.append(c)
    for c in first:
        c.wait_send()
    for k, c in enumerate(second):
        c.wait_send()
        if k >= 2:
            c.wait_recv()


def relayout(x, dest, count):
    vm = pl.BlockSpec(memory_space=pltpu.VMEM)
    return pl.pallas_call(
        relayout_kernel,
        out_shape=jax.ShapeDtypeStruct((704, 512), f32),
        in_specs=[pl.BlockSpec(memory_space=pl.ANY), vm, vm], out_specs=vm,
        scratch_shapes=[pltpu.VMEM((1024, 128), f32)] + [pltpu.VMEM((5, 72, 512), f32)] * 2
        + [pltpu.VMEM((3, 256, 512), bf16)]
        + [pltpu.SemaphoreType.DMA((5,))] * 2 + [pltpu.SemaphoreType.DMA((7,))] * 2 + [pltpu.SemaphoreType.DMA],
        compiler_params=pltpu.CompilerParams(collective_id=0, has_side_effects=True, vmem_limit_bytes=32 * 2**20),
        name="relayout",
    )(x, dest, count)


BACK = ((320, 64, (1, 1)), (384, 64, (1, -1)), (192, 128, (1, 0)), (0, 128, (0, 1)), (128, 64, (0, -1)))


def combine_kernel(sums, cells, dens, lap, got, own_cells, s1, r1, fsem):
    greet([(0, -1), (0, 1), (-1, 0), (-1, -1), (-1, 1)])
    fetch = pltpu.make_async_copy(cells.at[pl.ds(0, 256)], own_cells, fsem)
    fetch.start()
    copies = []
    for k, (row, rows, where) in enumerate(BACK):
        c = copy_to(sums.at[:, pl.ds(256 + row, rows)], got.at[:, pl.ds(row, rows)], s1.at[k], r1.at[k], where)
        c.start()
        copies.append(c)
    x0, _ = centre()
    fetch.wait()
    for c in copies:
        c.wait()
    own = lax.rsqrt(jnp.full((64, 128), 0.01, f32)) - 1.0
    lists = ((0, 192, 320), (256, 384), (64,), (128,))
    for q in range(4):
        rows = slice(64 * q, 64 * q + 64)
        n = sums[0, rows, :]
        s = sums[1, rows, :]
        for r in lists[q]:
            n = n + got[0, r:r + 64, :]
            s = s + got[1, r:r + 64, :]
        filled = own_cells[rows, 0:128] - x0 < 0.5 * SENT
        dens[rows, :] = jnp.where(filled, (n - own) / ref_density, 0.0)
        lap[rows, :] = jnp.where(filled, (s - own_cells[rows, 384:512] * n) / ref_density, 0.0)


def combine(sums, cells):
    vm = pl.BlockSpec(memory_space=pltpu.VMEM)
    return pl.pallas_call(
        combine_kernel,
        out_shape=[jax.ShapeDtypeStruct((256, 128), f32)] * 2,
        in_specs=[vm, pl.BlockSpec(memory_space=pl.ANY)], out_specs=[vm] * 2,
        scratch_shapes=[pltpu.VMEM((2, 448, 128), f32), pltpu.VMEM((256, 512), f32), pltpu.SemaphoreType.DMA((5,)), pltpu.SemaphoreType.DMA((5,)),
                        pltpu.SemaphoreType.DMA],
        compiler_params=pltpu.CompilerParams(collective_id=1, has_side_effects=True, vmem_limit_bytes=16 * 2**20),
        name="combine",
    )(sums, cells)


def local(incoming, dest, counts):
    cells = relayout(incoming.reshape(1024, 128), dest, counts)
    sums = compute(counts, cells)
    density, laplace = combine(sums, cells)
    return density.reshape(2, 2, 64, 128), laplace.reshape(2, 2, 64, 128)


def solution(mesh):
    in_specs = (P("slab", "dom", None, None), P("slab", "dom"), P("slab", "dom", None))
    out_specs = (P("slab", "dom", None, None), P("slab", "dom", None, None))
    return jax.shard_map(local, mesh=mesh, in_specs=in_specs, out_specs=out_specs, check_vma=False)
```

```python
import functools
import jax, jax.numpy as jnp
from jax import lax
from jax.experimental import pallas as pl
from jax.experimental.pallas import tpu as pltpu
from jax.sharding import PartitionSpec as P

f32, bf16 = jnp.float32, jnp.bfloat16
SENT = 100.0
ZP = 66
ref_density = 268.0825731
N_SLAB, N_DOM = 4, 32

OFFS = [(0, 0, 0), (0, 0, 1)] + [(dx, dy, dz) for dx, dy in ((0, 1), (1, -1), (1, 0), (1, 1)) for dz in (-1, 0, 1)]
NT = len(OFFS)
FR = 5


def split3(v):
    h = v.astype(bf16).astype(f32)
    r = v - h
    m = r.astype(bf16).astype(f32)
    return h, m, r - m


def split2(v):
    h = v.astype(bf16).astype(f32)
    m = (v - h).astype(bf16).astype(f32)
    return h, m, h + m


def left(h, m):
    return [-2.0 * h, -2.0 * h, -2.0 * m, -2.0 * m]


def right(h, m):
    return [h, m, h, m]


def build_cols(p_ref, row0, col, x0, y0, own_cell, b_ref, f_ref, stage, stage_a):
    @pl.loop(0, 8)
    def _(k):
        z0 = k * 8
        rows = pl.ds(pl.multiple_of(row0 + z0, 8), 8)
        zc = (lax.broadcasted_iota(jnp.int32, (8, 128), 0) + z0).astype(f32) + 0.5
        xh, xm, x = split2(p_ref[rows, 0:128] - x0)
        yh, ym, y = split2(p_ref[rows, 128:256] - y0)
        zh, zm, z = split2(p_ref[rows, 256:384] - zc)
        f = p_ref[rows, 384:512]
        f_ref[pl.ds(col * ZP + 1 + z0, 8), :] = f
        xy = x * x + y * y
        terms = dict(enumerate(right(xh, xm) + right(yh, ym) + list(split3(xy + z * z))))
        terms.update(enumerate(right(zh, zm), 16))
        for r, v in terms.items():
            stage[pl.ds(r, 8, stride=32), :] = v
        b_ref[pl.ds(pl.multiple_of((col * ZP + 1 + z0) * 32, 32), 256), :] = stage[...].astype(bf16)
        if own_cell is None:
            return
        terms = dict(enumerate(left(xh, xm) + left(yh, ym)))
        for k2, s in enumerate((-1.0, 0.0, 1.0)):
            h, m, zs = split2(z - s)
            terms.update(enumerate(left(h, m) + list(split3(xy + zs * zs)), 16 + 16 * k2))
        terms.update(enumerate(split3(f), 23))
        for r, v in terms.items():
            stage_a[pl.ds((own_cell + z0) * 64 + r, 8, stride=64), :] = v


def cell_of(cell):
    cell = jnp.asarray(cell, jnp.int32)
    cx, cy, z = cell >> 7, (cell >> 6) & 1, cell & 63
    return (cx * 4 + cy + 1) * ZP + 1 + z


STEPS = [(dx * 4 + dy) * ZP + dz for dx, dy, dz in OFFS]


def rows_of(base, count):
    first = base * count
    return [pl.ds(pl.multiple_of(first + step * count, count), count) for step in STEPS]


def turn(cell, a_ref, stage_a):
    a_ref[...] = stage_a[pl.ds(pl.multiple_of(cell * 64, 64), 64), :].T.astype(bf16)


def make_d(cell, d_ref, a_ref, b_ref):
    a = a_ref[...]
    zero = jnp.zeros((16, 128), bf16)
    ri = lax.broadcasted_iota(jnp.int32, (16, 128), 0)
    pick = jnp.where((ri >= 7) & (ri < 10), 1.0, 0.0).astype(bf16)
    ws = []
    for (dx, dy, dz), rows in zip(OFFS, rows_of(cell_of(cell), 32)):
        b = b_ref[rows, :]
        ws.append(jnp.concatenate([b[:16]] + [b[16:] if k == dz else zero for k in (-1, 0, 1)], 0))
    ws.append(jnp.concatenate([zero, pick, zero, zero], 0))

    def part(t, r):
        w = jnp.concatenate(ws[t:t + 2], 1)
        d_ref[r:r + 32, 128 * t:128 * t + w.shape[1]] = jnp.dot(a[r:r + 32], w, preferred_element_type=f32)
    return [functools.partial(part, t, r) for t in range(0, NT + 1, 2) for r in range(0, 128, 32)]


def finish(cell, an_ref, as_ref, out_ref):
    out_ref[0, pl.ds(cell, 1), :] = jnp.sum(an_ref[...].T, axis=0, keepdims=True)
    out_ref[1, pl.ds(cell, 1), :] = jnp.sum(as_ref[...].T, axis=0, keepdims=True)


def pair_sums(R, cell, d_ref, an_ref, as_ref, f_ref, jn_ref, js_ref, parts):
    if R == 0:
        for part in parts:
            part()
        return
    base = cell_of(cell)
    fj = [jnp.broadcast_to(f_ref[pl.ds(base + step, 1), :], (8, 128)) for step in STEPS]
    f0 = fj[0]
    for v in fj[1:]:
        f0 = f0 + v
    cn = [jnp.full((8, 128), -(R // 8.0), f32) for _ in STEPS]
    fi0 = d_ref[0:8, 128 * NT:128 * NT + 128]
    for r in range(8, R, 8):
        fi0 = fi0 + d_ref[r:r + 8, 128 * NT:128 * NT + 128]
    cm = [-fi0 for _ in STEPS]
    for r in range(0, R, 8):
        fi = d_ref[r:r + 8, 128 * NT:128 * NT + 128]
        an = jnp.full((8, 128), -float(NT), f32)
        am = -f0
        for t in range(NT):
            d = d_ref[r:r + 8, 128 * t:128 * t + 128]
            q = jnp.maximum(lax.rsqrt(jnp.maximum(d, 0.01)), 1.0)
            an = an + q
            am = am + q * fj[t]
            if t:
                cn[t] = cn[t] + q
                cm[t] = cm[t] + q * fi
        an_ref[r:r + 8, :] = an
        as_ref[r:r + 8, :] = am
        for part in parts[min(FR * r * len(parts) // R // 4, len(parts)):min(FR * (r + 8) * len(parts) // R // 4, len(parts))]:
            part()
    rows = rows_of(base, 8)
    olds = [(jn_ref[rows[t], :], js_ref[rows[t], :]) for t in range(1, NT)]
    for t in range(1, NT):
        jn_ref[rows[t], :] = olds[t - 1][0] + cn[t]
        js_ref[rows[t], :] = olds[t - 1][1] + cm[t]


def tree(v, lo, hi, run):
    if hi - lo == 1:
        run(lo)
        return
    mid = (lo + hi) // 2

    @pl.when(v < mid)
    def _():
        tree(v, lo, mid, run)

    @pl.when(v >= mid)
    def _():
        tree(v, mid, hi, run)


def centre():
    return (lax.axis_index("slab") * 2 + 1).astype(f32), (lax.axis_index("dom") * 2 + 1).astype(f32)


def kern(cnt_ref, cells, out_ref,
         a0, a1, b_ref, f_ref, jn_ref, js_ref, stage, stage_a, d0, d1, an0, as0, an1, as1):
    x0, y0 = centre()
    ra = lax.broadcasted_iota(jnp.int32, (64, 128), 0)
    ones = jnp.where((ra >= 8) & (ra < 11), 1.0, 0.0)

    @pl.loop(0, 32)
    def _(k):
        for j in range(8):
            stage_a[pl.ds(pl.multiple_of(k * 512 + 64 * j, 64), 64), :] = ones
    rb = lax.broadcasted_iota(jnp.int32, stage.shape, 0) % 32
    stage[...] = jnp.where((rb >= 20) & (rb < 23), 1.0, 0.0)
    ri = lax.broadcasted_iota(jnp.int32, (32, 128), 0)
    rim = (jnp.where(ri == 8, SENT * SENT, 0.0) + jnp.where((ri >= 20) & (ri < 23), 1.0, 0.0)).astype(bf16)

    @pl.loop(0, 12)
    def _(col):
        for zz in (0, ZP - 1):
            b_ref[pl.ds(pl.multiple_of((col * ZP + zz) * 32, 32), 32), :] = rim
            f_ref[pl.ds(col * ZP + zz, 1), :] = jnp.zeros((1, 128), f32)

    @pl.loop(0, 12)
    def _(k):
        rows = pl.ds(pl.multiple_of(k * 8 * ZP, 8), 8 * ZP)
        jn_ref[rows, :] = jnp.zeros((8 * ZP, 128), f32)
        js_ref[rows, :] = jnp.zeros((8 * ZP, 128), f32)

    b = functools.partial(build_cols, x0=x0, y0=y0, b_ref=b_ref, f_ref=f_ref, stage=stage, stage_a=stage_a)

    @pl.loop(0, 4)
    def _(k):
        b(cells, k * 64, (k // 2) * 4 + k % 2 + 1, own_cell=k * 64)

    @pl.loop(0, 7)
    def _(k):
        col = jnp.where(k < 2, 3 + 4 * k, jnp.where(k < 3, 4, jnp.where(k < 6, 6 + k, 8)))
        b(cells, 256 + k * 64, col, own_cell=None)

    turn(0, a0, stage_a)
    turn(1, a1, stage_a)
    for part in make_d(0, d0, a0, b_ref):
        part()
    bufs = ((d0, an0, as0, a0), (d1, an1, as1, a1))

    @pl.loop(0, 128)
    def _(i):
        for p in range(2):
            cell = i * 2 + p
            nxt = jnp.minimum(cell + 1, 255)
            prev = jnp.maximum(cell - 1, 0)
            d, an, am, a = bufs[p]
            dn, anp, amp, a_next = bufs[1 - p]
            later = jnp.minimum(cell + 2, 255)

            def run(k):
                turn(later, a, stage_a)
                parts = make_d(nxt, dn, a_next, b_ref)
                finish(prev, anp, amp, out_ref)
                pair_sums(16 * k, cell, d, an, am, f_ref, jn_ref, js_ref, parts)
            tree((cnt_ref[cell >> 7, (cell >> 6) & 1, cell & 63] + 15) >> 4, 0, 9, run)
    finish(255, an1, as1, out_ref)

    def side(col, z0, ref):
        base = (col * ZP + 1 + z0) * 8
        v = ref[pl.ds(base, 8, stride=8), :]
        for k in range(1, 8):
            v = v + ref[pl.ds(base + k, 8, stride=8), :]
        return v

    @pl.loop(0, 32)
    def _(k):
        cx, cy, z0 = k // 16, (k // 8) % 2, (k % 8) * 8
        rows = pl.ds(pl.multiple_of(k * 8, 8), 8)
        out_ref[0, rows, :] += side(cx * 4 + cy + 1, z0, jn_ref)
        out_ref[1, rows, :] += side(cx * 4 + cy + 1, z0, js_ref)

    @pl.loop(0, 8)
    def _(k):
        for h, col in enumerate((3, 7, 4, 9, 10, 11, 8)):
            rows = pl.ds(pl.multiple_of(256 + h * 64 + k * 8, 8), 8)
            out_ref[0, rows, :] = side(col, k * 8, jn_ref)
            out_ref[1, rows, :] = side(col, k * 8, js_ref)


def compute(cnt, cells):
    vm = pl.BlockSpec(memory_space=pltpu.VMEM)
    sm = pl.BlockSpec(memory_space=pltpu.SMEM)
    return pl.pallas_call(
        kern,
        out_shape=jax.ShapeDtypeStruct((2, 704, 128), f32),
        in_specs=[sm, vm], out_specs=vm,
        scratch_shapes=[pltpu.VMEM((128, 64), bf16), pltpu.VMEM((128, 64), bf16), pltpu.VMEM((12 * ZP * 32, 128), bf16),
                        pltpu.VMEM((12 * ZP, 128), f32), pltpu.VMEM((12 * ZP * 8, 128), f32), pltpu.VMEM((12 * ZP * 8, 128), f32),
                        pltpu.VMEM((256, 128), f32), pltpu.VMEM((256 * 64, 128), f32)]
        + [pltpu.VMEM((128, 128 * (NT + 1)), f32)] * 2 + [pltpu.VMEM((128, 128), f32)] * 4,
        compiler_params=pltpu.CompilerParams(vmem_limit_bytes=30 * 2**20),
        name="pairs",
    )(cnt, cells)


def far(ds, dd):
    slab = lax.rem(lax.axis_index("slab") + (ds + N_SLAB), N_SLAB)
    dom = lax.rem(lax.axis_index("dom") + (dd + N_DOM), N_DOM)
    return (slab, dom)


def copy_to(src, dst, send, recv, where):
    return pltpu.make_async_remote_copy(
        src_ref=src, dst_ref=dst, send_sem=send, recv_sem=recv, device_id=far(*where),
        device_id_type=pl.DeviceIdType.MESH)


def greet(senders):
    barrier = pltpu.get_barrier_semaphore()
    for where in senders:
        pl.semaphore_signal(barrier, inc=1, device_id=far(*where), device_id_type=pl.DeviceIdType.MESH)
    pl.semaphore_wait(barrier, len(senders))


def picked(onehot, v, dims):
    out = None
    for part in reversed(split3(v)):
        p = lax.dot_general(onehot, part.astype(bf16), (dims, ((), ())), preferred_element_type=f32)
        out = p if out is None else out + p
    return out


def iota(shape, dim):
    return lax.broadcasted_iota(jnp.int32, shape, dim).astype(f32)


FAR = (0, 4, 1, 3)
HALO = ((0, 64, (-1, 0), 448), (64, 64, (-1, 0), 512), (0, 64, (0, -1), 256), (128, 64, (0, -1), 320),
        (192, 64, (0, 1), 384), (448, 64, (0, -1), 576), (512, 64, (0, 1), 640))


def relayout_kernel(x_any, dest_ref, cnt_ref, cells, x_ref, sent, got, parts, s1, r1, s2, r2, xsem):
    fetch = pltpu.make_async_copy(x_any, x_ref, xsem)
    fetch.start()
    me = lax.axis_index("dom")
    greet([(0, -2), (0, -1), (0, 1), (0, 2), (1, 0)])
    dest = dest_ref[...]
    dom = lax.shift_right_logical(dest, 8)
    shift = (dom - me).astype(f32)
    shift = jnp.where(shift < -16.0, shift + 32.0, jnp.where(shift > 16.0, shift - 32.0, shift)) + 2.0
    local = (dest - dom * 256).astype(f32)
    chosen = jnp.where(iota((8, 256), 0) == shift, 1.0, 0.0)
    lower = jnp.where(iota((256, 256), 0) <= iota((256, 256), 1), 1.0, 0.0).astype(bf16)
    rank = jnp.dot(chosen.astype(bf16), lower, preferred_element_type=f32)
    rank = jnp.sum(chosen * rank, axis=0, keepdims=True) - 1.0
    slot = shift * 64.0 + rank
    tag = jnp.broadcast_to(local + 1.0, (8, 256)).astype(bf16)
    fetch.wait()
    for c in range(4):
        for p, v in enumerate(split3(x_ref[pl.ds(c, 256, stride=4), :])):
            parts[p, :, 128 * c:128 * c + 128] = v.astype(bf16)

    def send_part(k, dst):
        pack = jnp.where(iota((64, 256), 0) + 64.0 * k == slot, 1.0, 0.0).astype(bf16)
        out = [jnp.dot(pack, parts[p], preferred_element_type=f32) for p in (2, 1, 0)]
        dst[k, 0:64, :] = out[0] + out[1] + out[2]
        dst[k, 64:72, 0:64] = lax.dot_general(tag, pack, (((1,), (1,)), ((), ())), preferred_element_type=f32)
    sent[:, 64:72, :] = jnp.zeros((5, 8, 512), f32)
    first = []
    for k in FAR:
        send_part(k, sent)
        c = copy_to(sent.at[k], got.at[k], s1.at[k], r1.at[k], (0, k - 2))
        c.start()
        first.append(c)
    send_part(2, got)
    diag = jnp.where(iota((256, 256), 0) == iota((256, 256), 1), 1.0, 0.0)
    count = jnp.concatenate([cnt_ref[a, b:b + 1, :] for a in range(2) for b in range(2)], 1).astype(f32)
    count = jnp.sum(diag * count, axis=1, keepdims=True)
    filled = iota((256, 128), 1) < count
    for c in first:
        c.wait_recv()
    label = jnp.concatenate([got[k, 64:65, 0:64] for k in range(5)], 1)
    place = jnp.where(iota((256, 320), 0) + 1.0 == label, 1.0, 0.0).astype(bf16)
    total = picked(place, jnp.concatenate([got[k, 0:64, :] for k in range(5)], 0), ((1,), (0,)))
    x0, _ = centre()
    cells[0:256, 0:128] = jnp.where(filled, total[:, 0:128], x0 + SENT)
    cells[0:256, 128:384] = total[:, 128:384]
    cells[0:256, 384:512] = jnp.where(filled, total[:, 384:512], 0.0)
    second = []
    for k, (row, rows, where, there) in enumerate(HALO):
        if k >= 5:
            second[k - 5].wait_recv()
        c = copy_to(cells.at[pl.ds(row, rows)], cells.at[pl.ds(there, rows)], s2.at[k], r2.at[k], where)
        c.start()
        second.append(c)
    for c in first:
        c.wait_send()
    for k, c in enumerate(second):
        c.wait_send()
        if k >= 2:
            c.wait_recv()


def relayout(x, dest, count):
    vm = pl.BlockSpec(memory_space=pltpu.VMEM)
    return pl.pallas_call(
        relayout_kernel,
        out_shape=jax.ShapeDtypeStruct((704, 512), f32),
        in_specs=[pl.BlockSpec(memory_space=pl.ANY), vm, vm], out_specs=vm,
        scratch_shapes=[pltpu.VMEM((1024, 128), f32)] + [pltpu.VMEM((5, 72, 512), f32)] * 2
        + [pltpu.VMEM((3, 256, 512), bf16)]
        + [pltpu.SemaphoreType.DMA((5,))] * 2 + [pltpu.SemaphoreType.DMA((7,))] * 2 + [pltpu.SemaphoreType.DMA],
        compiler_params=pltpu.CompilerParams(collective_id=0, has_side_effects=True, vmem_limit_bytes=56 * 2**20),
        name="relayout",
    )(x, dest, count)


BACK = ((320, 64, (1, 1)), (384, 64, (1, -1)), (192, 128, (1, 0)), (0, 128, (0, 1)), (128, 64, (0, -1)))


def combine_kernel(sums, cells, dens, lap, got, own_cells, s1, r1, fsem):
    greet([(0, -1), (0, 1), (-1, 0), (-1, -1), (-1, 1)])
    fetch = pltpu.make_async_copy(cells.at[pl.ds(0, 256)], own_cells, fsem)
    fetch.start()
    copies = []
    for k, (row, rows, where) in enumerate(BACK):
        c = copy_to(sums.at[:, pl.ds(256 + row, rows)], got.at[:, pl.ds(row, rows)], s1.at[k], r1.at[k], where)
        c.start()
        copies.append(c)
    x0, _ = centre()
    fetch.wait()
    for c in copies:
        c.wait()
    own = lax.rsqrt(jnp.full((64, 128), 0.01, f32)) - 1.0
    lists = ((0, 192, 320), (256, 384), (64,), (128,))
    for q in range(4):
        rows = slice(64 * q, 64 * q + 64)
        n = sums[0, rows, :]
        s = sums[1, rows, :]
        for r in lists[q]:
            n = n + got[0, r:r + 64, :]
            s = s + got[1, r:r + 64, :]
        filled = own_cells[rows, 0:128] - x0 < 0.5 * SENT
        dens[rows, :] = jnp.where(filled, (n - own) / ref_density, 0.0)
        lap[rows, :] = jnp.where(filled, (s - own_cells[rows, 384:512] * n) / ref_density, 0.0)


def combine(sums, cells):
    vm = pl.BlockSpec(memory_space=pltpu.VMEM)
    return pl.pallas_call(
        combine_kernel,
        out_shape=[jax.ShapeDtypeStruct((256, 128), f32)] * 2,
        in_specs=[vm, pl.BlockSpec(memory_space=pl.ANY)], out_specs=[vm] * 2,
        scratch_shapes=[pltpu.VMEM((2, 448, 128), f32), pltpu.VMEM((256, 512), f32), pltpu.SemaphoreType.DMA((5,)), pltpu.SemaphoreType.DMA((5,)),
                        pltpu.SemaphoreType.DMA],
        compiler_params=pltpu.CompilerParams(collective_id=1, has_side_effects=True, vmem_limit_bytes=16 * 2**20),
        name="combine",
    )(sums, cells)


def local(incoming, dest, counts):
    cells = relayout(incoming.reshape(1024, 128), dest, counts)
    sums = compute(counts, cells)
    density, laplace = combine(sums, cells)
    return density.reshape(2, 2, 64, 128), laplace.reshape(2, 2, 64, 128)


def solution(mesh):
    in_specs = (P("slab", "dom", None, None), P("slab", "dom"), P("slab", "dom", None))
    out_specs = (P("slab", "dom", None, None), P("slab", "dom", None, None))
    return jax.shard_map(local, mesh=mesh, in_specs=in_specs, out_specs=out_specs, check_vma=False)
```

```python
import functools
import jax, jax.numpy as jnp
from jax import lax
from jax.experimental import pallas as pl
from jax.experimental.pallas import tpu as pltpu
from jax.sharding import PartitionSpec as P

f32, bf16 = jnp.float32, jnp.bfloat16
SENT = 100.0
ZP = 66
ref_density = 268.0825731
N_SLAB, N_DOM = 4, 32

OFFS = [(0, 0, 0), (0, 0, 1)] + [(dx, dy, dz) for dx, dy in ((0, 1), (1, -1), (1, 0), (1, 1)) for dz in (-1, 0, 1)]
NT = len(OFFS)
FR = 5


def split3(v):
    h = v.astype(bf16).astype(f32)
    r = v - h
    m = r.astype(bf16).astype(f32)
    return h, m, r - m


def split2(v):
    h = v.astype(bf16).astype(f32)
    m = (v - h).astype(bf16).astype(f32)
    return h, m, h + m


def left(h, m):
    return [-2.0 * h, -2.0 * h, -2.0 * m, -2.0 * m]


def right(h, m):
    return [h, m, h, m]


def build_cols(p_ref, row0, col, x0, y0, own_cell, b_ref, f_ref, stage, stage_a):
    @pl.loop(0, 8)
    def _(k):
        z0 = k * 8
        rows = pl.ds(pl.multiple_of(row0 + z0, 8), 8)
        zc = (lax.broadcasted_iota(jnp.int32, (8, 128), 0) + z0).astype(f32) + 0.5
        xh, xm, x = split2(p_ref[rows, 0:128] - x0)
        yh, ym, y = split2(p_ref[rows, 128:256] - y0)
        zh, zm, z = split2(p_ref[rows, 256:384] - zc)
        f = p_ref[rows, 384:512]
        f_ref[pl.ds(col * ZP + 1 + z0, 8), :] = f
        xy = x * x + y * y
        terms = dict(enumerate(right(xh, xm) + right(yh, ym) + list(split3(xy + z * z))))
        terms.update(enumerate(right(zh, zm), 16))
        for r, v in terms.items():
            stage[pl.ds(r, 8, stride=32), :] = v
        b_ref[pl.ds(pl.multiple_of((col * ZP + 1 + z0) * 32, 32), 256), :] = stage[...].astype(bf16)
        if own_cell is None:
            return
        terms = dict(enumerate(left(xh, xm) + left(yh, ym)))
        for k2, s in enumerate((-1.0, 0.0, 1.0)):
            h, m, zs = split2(z - s)
            terms.update(enumerate(left(h, m) + list(split3(xy + zs * zs)), 16 + 16 * k2))
        terms.update(enumerate(split3(f), 23))
        for r, v in terms.items():
            stage_a[pl.ds((own_cell + z0) * 64 + r, 8, stride=64), :] = v


def cell_of(cell):
    cell = jnp.asarray(cell, jnp.int32)
    cx, cy, z = cell >> 7, (cell >> 6) & 1, cell & 63
    return (cx * 4 + cy + 1) * ZP + 1 + z


STEPS = [(dx * 4 + dy) * ZP + dz for dx, dy, dz in OFFS]


def rows_of(base, count):
    first = base * count
    return [pl.ds(pl.multiple_of(first + step * count, count), count) for step in STEPS]


def turn(cell, a_ref, stage_a):
    a_ref[...] = stage_a[pl.ds(pl.multiple_of(cell * 64, 64), 64), :].T.astype(bf16)


def make_d(cell, d_ref, a_ref, b_ref):
    a = a_ref[...]
    zero = jnp.zeros((16, 128), bf16)
    ri = lax.broadcasted_iota(jnp.int32, (16, 128), 0)
    pick = jnp.where((ri >= 7) & (ri < 10), 1.0, 0.0).astype(bf16)
    ws = []
    for (dx, dy, dz), rows in zip(OFFS, rows_of(cell_of(cell), 32)):
        b = b_ref[rows, :]
        ws.append(jnp.concatenate([b[:16]] + [b[16:] if k == dz else zero for k in (-1, 0, 1)], 0))
    ws.append(jnp.concatenate([zero, pick, zero, zero], 0))

    def part(t, r):
        w = jnp.concatenate(ws[t:t + 2], 1)
        d_ref[r:r + 32, 128 * t:128 * t + w.shape[1]] = jnp.dot(a[r:r + 32], w, preferred_element_type=f32)
    return [functools.partial(part, t, r) for t in range(0, NT + 1, 2) for r in range(0, 128, 32)]


def finish(cell, an_ref, as_ref, out_ref):
    out_ref[0, pl.ds(cell, 1), :] = jnp.sum(an_ref[...].T, axis=0, keepdims=True)
    out_ref[1, pl.ds(cell, 1), :] = jnp.sum(as_ref[...].T, axis=0, keepdims=True)


def pair_sums(R, cell, d_ref, an_ref, as_ref, f_ref, jn_ref, js_ref, parts):
    if R == 0:
        for part in parts:
            part()
        return
    base = cell_of(cell)
    fj = [jnp.broadcast_to(f_ref[pl.ds(base + step, 1), :], (8, 128)) for step in STEPS]
    f0 = fj[0]
    for v in fj[1:]:
        f0 = f0 + v
    cn = [jnp.full((8, 128), -(R // 8.0), f32) for _ in STEPS]
    fi0 = d_ref[0:8, 128 * NT:128 * NT + 128]
    for r in range(8, R, 8):
        fi0 = fi0 + d_ref[r:r + 8, 128 * NT:128 * NT + 128]
    cm = [-fi0 for _ in STEPS]
    for r in range(0, R, 8):
        fi = d_ref[r:r + 8, 128 * NT:128 * NT + 128]
        an = jnp.full((8, 128), -float(NT), f32)
        am = -f0
        for t in range(NT):
            d = d_ref[r:r + 8, 128 * t:128 * t + 128]
            q = jnp.maximum(lax.rsqrt(jnp.maximum(d, 0.01)), 1.0)
            an = an + q
            am = am + q * fj[t]
            if t:
                cn[t] = cn[t] + q
                cm[t] = cm[t] + q * fi
        an_ref[r:r + 8, :] = an
        as_ref[r:r + 8, :] = am
        for part in parts[min(FR * r * len(parts) // R // 4, len(parts)):min(FR * (r + 8) * len(parts) // R // 4, len(parts))]:
            part()
    rows = rows_of(base, 8)
    olds = [(jn_ref[rows[t], :], js_ref[rows[t], :]) for t in range(1, NT)]
    for t in range(1, NT):
        jn_ref[rows[t], :] = olds[t - 1][0] + cn[t]
        js_ref[rows[t], :] = olds[t - 1][1] + cm[t]


def tree(v, lo, hi, run):
    if hi - lo == 1:
        run(lo)
        return
    mid = (lo + hi) // 2

    @pl.when(v < mid)
    def _():
        tree(v, lo, mid, run)

    @pl.when(v >= mid)
    def _():
        tree(v, mid, hi, run)


def centre():
    return (lax.axis_index("slab") * 2 + 1).astype(f32), (lax.axis_index("dom") * 2 + 1).astype(f32)


def kern(cnt_ref, cells, out_ref,
         a0, a1, b_ref, f_ref, jn_ref, js_ref, stage, stage_a, d0, d1, an0, as0, an1, as1):
    x0, y0 = centre()
    ra = lax.broadcasted_iota(jnp.int32, (64, 128), 0)
    ones = jnp.where((ra >= 8) & (ra < 11), 1.0, 0.0)

    @pl.loop(0, 32)
    def _(k):
        for j in range(8):
            stage_a[pl.ds(pl.multiple_of(k * 512 + 64 * j, 64), 64), :] = ones
    rb = lax.broadcasted_iota(jnp.int32, stage.shape, 0) % 32
    stage[...] = jnp.where((rb >= 20) & (rb < 23), 1.0, 0.0)
    ri = lax.broadcasted_iota(jnp.int32, (32, 128), 0)
    rim = (jnp.where(ri == 8, SENT * SENT, 0.0) + jnp.where((ri >= 20) & (ri < 23), 1.0, 0.0)).astype(bf16)

    @pl.loop(0, 12)
    def _(col):
        for zz in (0, ZP - 1):
            b_ref[pl.ds(pl.multiple_of((col * ZP + zz) * 32, 32), 32), :] = rim
            f_ref[pl.ds(col * ZP + zz, 1), :] = jnp.zeros((1, 128), f32)

    @pl.loop(0, 12)
    def _(k):
        rows = pl.ds(pl.multiple_of(k * 8 * ZP, 8), 8 * ZP)
        jn_ref[rows, :] = jnp.zeros((8 * ZP, 128), f32)
        js_ref[rows, :] = jnp.zeros((8 * ZP, 128), f32)

    b = functools.partial(build_cols, x0=x0, y0=y0, b_ref=b_ref, f_ref=f_ref, stage=stage, stage_a=stage_a)

    @pl.loop(0, 4)
    def _(k):
        b(cells, k * 64, (k // 2) * 4 + k % 2 + 1, own_cell=k * 64)

    @pl.loop(0, 7)
    def _(k):
        col = jnp.where(k < 2, 3 + 4 * k, jnp.where(k < 3, 4, jnp.where(k < 6, 6 + k, 8)))
        b(cells, 256 + k * 64, col, own_cell=None)

    turn(0, a0, stage_a)
    turn(1, a1, stage_a)
    for part in make_d(0, d0, a0, b_ref):
        part()
    bufs = ((d0, an0, as0, a0), (d1, an1, as1, a1))

    @pl.loop(0, 128)
    def _(i):
        for p in range(2):
            cell = i * 2 + p
            nxt = jnp.minimum(cell + 1, 255)
            prev = jnp.maximum(cell - 1, 0)
            d, an, am, a = bufs[p]
            dn, anp, amp, a_next = bufs[1 - p]
            later = jnp.minimum(cell + 2, 255)

            def run(k):
                turn(later, a, stage_a)
                parts = make_d(nxt, dn, a_next, b_ref)
                finish(prev, anp, amp, out_ref)
                pair_sums(16 * k, cell, d, an, am, f_ref, jn_ref, js_ref, parts)
            tree((cnt_ref[cell >> 7, (cell >> 6) & 1, cell & 63] + 15) >> 4, 0, 9, run)
    finish(255, an1, as1, out_ref)

    def side(col, z0, ref):
        base = (col * ZP + 1 + z0) * 8
        v = ref[pl.ds(base, 8, stride=8), :]
        for k in range(1, 8):
            v = v + ref[pl.ds(base + k, 8, stride=8), :]
        return v

    @pl.loop(0, 32)
    def _(k):
        cx, cy, z0 = k // 16, (k // 8) % 2, (k % 8) * 8
        rows = pl.ds(pl.multiple_of(k * 8, 8), 8)
        out_ref[0, rows, :] += side(cx * 4 + cy + 1, z0, jn_ref)
        out_ref[1, rows, :] += side(cx * 4 + cy + 1, z0, js_ref)

    @pl.loop(0, 8)
    def _(k):
        for h, col in enumerate((3, 7, 4, 9, 10, 11, 8)):
            rows = pl.ds(pl.multiple_of(256 + h * 64 + k * 8, 8), 8)
            out_ref[0, rows, :] = side(col, k * 8, jn_ref)
            out_ref[1, rows, :] = side(col, k * 8, js_ref)


def compute(cnt, cells):
    vm = pl.BlockSpec(memory_space=pltpu.VMEM)
    sm = pl.BlockSpec(memory_space=pltpu.SMEM)
    return pl.pallas_call(
        kern,
        out_shape=jax.ShapeDtypeStruct((2, 704, 128), f32),
        in_specs=[sm, vm], out_specs=vm,
        scratch_shapes=[pltpu.VMEM((128, 64), bf16), pltpu.VMEM((128, 64), bf16), pltpu.VMEM((12 * ZP * 32, 128), bf16),
                        pltpu.VMEM((12 * ZP, 128), f32), pltpu.VMEM((12 * ZP * 8, 128), f32), pltpu.VMEM((12 * ZP * 8, 128), f32),
                        pltpu.VMEM((256, 128), f32), pltpu.VMEM((256 * 64, 128), f32)]
        + [pltpu.VMEM((128, 128 * (NT + 1)), f32)] * 2 + [pltpu.VMEM((128, 128), f32)] * 4,
        compiler_params=pltpu.CompilerParams(vmem_limit_bytes=30 * 2**20),
        name="pairs",
    )(cnt, cells)


def far(ds, dd):
    slab = lax.rem(lax.axis_index("slab") + (ds + N_SLAB), N_SLAB)
    dom = lax.rem(lax.axis_index("dom") + (dd + N_DOM), N_DOM)
    return (slab, dom)


def copy_to(src, dst, send, recv, where):
    return pltpu.make_async_remote_copy(
        src_ref=src, dst_ref=dst, send_sem=send, recv_sem=recv, device_id=far(*where),
        device_id_type=pl.DeviceIdType.MESH)


def greet(senders):
    barrier = pltpu.get_barrier_semaphore()
    for where in senders:
        pl.semaphore_signal(barrier, inc=1, device_id=far(*where), device_id_type=pl.DeviceIdType.MESH)
    pl.semaphore_wait(barrier, len(senders))


def picked(onehot, v, dims):
    out = None
    for part in reversed(split3(v)):
        p = lax.dot_general(onehot, part.astype(bf16), (dims, ((), ())), preferred_element_type=f32)
        out = p if out is None else out + p
    return out


def iota(shape, dim):
    return lax.broadcasted_iota(jnp.int32, shape, dim).astype(f32)


FAR = (0, 4, 1, 3)
HALO = ((0, 64, (-1, 0), 448), (64, 64, (-1, 0), 512), (0, 64, (0, -1), 256), (128, 64, (0, -1), 320),
        (192, 64, (0, 1), 384), (448, 64, (0, -1), 576), (512, 64, (0, 1), 640))


def relayout_kernel(x_any, dest_ref, cnt_ref, cells, x_ref, sent, got, parts, s1, r1, s2, r2, xsem):
    fetch = pltpu.make_async_copy(x_any, x_ref, xsem)
    fetch.start()
    me = lax.axis_index("dom")
    greet([(0, -2), (0, -1), (0, 1), (0, 2), (1, 0)])
    dest = dest_ref[...]
    dom = lax.shift_right_logical(dest, 8)
    shift = (dom - me).astype(f32)
    shift = jnp.where(shift < -16.0, shift + 32.0, jnp.where(shift > 16.0, shift - 32.0, shift)) + 2.0
    local = (dest - dom * 256).astype(f32)
    chosen = jnp.where(iota((8, 256), 0) == shift, 1.0, 0.0)
    lower = jnp.where(iota((256, 256), 0) <= iota((256, 256), 1), 1.0, 0.0).astype(bf16)
    rank = jnp.dot(chosen.astype(bf16), lower, preferred_element_type=f32)
    rank = jnp.sum(chosen * rank, axis=0, keepdims=True) - 1.0
    slot = shift * 64.0 + rank
    tag = jnp.broadcast_to(local + 1.0, (8, 256)).astype(bf16)
    fetch.wait()
    for c in range(4):
        for p, v in enumerate(split3(x_ref[pl.ds(c, 256, stride=4), :])):
            parts[p, :, 128 * c:128 * c + 128] = v.astype(bf16)

    def send_part(k, dst):
        pack = jnp.where(iota((64, 256), 0) + 64.0 * k == slot, 1.0, 0.0).astype(bf16)
        out = [jnp.dot(pack, parts[p], preferred_element_type=f32) for p in (2, 1, 0)]
        dst[k, 0:64, :] = out[0] + out[1] + out[2]
        dst[k, 64:72, 0:64] = lax.dot_general(tag, pack, (((1,), (1,)), ((), ())), preferred_element_type=f32)
    sent[:, 64:72, :] = jnp.zeros((5, 8, 512), f32)
    first = []
    for k in FAR:
        send_part(k, sent)
        c = copy_to(sent.at[k], got.at[k], s1.at[k], r1.at[k], (0, k - 2))
        c.start()
        first.append(c)
    send_part(2, got)
    diag = jnp.where(iota((256, 256), 0) == iota((256, 256), 1), 1.0, 0.0)
    count = jnp.concatenate([cnt_ref[a, b:b + 1, :] for a in range(2) for b in range(2)], 1).astype(f32)
    count = jnp.sum(diag * count, axis=1, keepdims=True)
    filled = iota((256, 128), 1) < count
    for c in first:
        c.wait_recv()
    label = jnp.concatenate([got[k, 64:65, 0:64] for k in range(5)], 1)
    data = jnp.concatenate([got[k, 0:64, :] for k in range(5)], 0)
    x0, _ = centre()
    second = []
    for half in range(2):
        a, b = 128 * half, 128 * half + 128
        place = jnp.where(iota((128, 320), 0) + (1.0 + a) == label, 1.0, 0.0).astype(bf16)
        total = picked(place, data, ((1,), (0,)))
        cells[a:b, 0:128] = jnp.where(filled[a:b], total[:, 0:128], x0 + SENT)
        cells[a:b, 128:384] = total[:, 128:384]
        cells[a:b, 384:512] = jnp.where(filled[a:b], total[:, 384:512], 0.0)
        for k in ((0, 1, 2) if half == 0 else (3, 4, 5, 6)):
            row, rows, where, there = HALO[k]
            if k >= 5:
                second[k - 5].wait_recv()
            c = copy_to(cells.at[pl.ds(row, rows)], cells.at[pl.ds(there, rows)], s2.at[k], r2.at[k], where)
            c.start()
            second.append(c)
    for c in first:
        c.wait_send()
    for k, c in enumerate(second):
        c.wait_send()
        if k >= 2:
            c.wait_recv()


def relayout(x, dest, count):
    vm = pl.BlockSpec(memory_space=pltpu.VMEM)
    return pl.pallas_call(
        relayout_kernel,
        out_shape=jax.ShapeDtypeStruct((704, 512), f32),
        in_specs=[pl.BlockSpec(memory_space=pl.ANY), vm, vm], out_specs=vm,
        scratch_shapes=[pltpu.VMEM((1024, 128), f32)] + [pltpu.VMEM((5, 72, 512), f32)] * 2
        + [pltpu.VMEM((3, 256, 512), bf16)]
        + [pltpu.SemaphoreType.DMA((5,))] * 2 + [pltpu.SemaphoreType.DMA((7,))] * 2 + [pltpu.SemaphoreType.DMA],
        compiler_params=pltpu.CompilerParams(collective_id=0, has_side_effects=True, vmem_limit_bytes=32 * 2**20),
        name="relayout",
    )(x, dest, count)


BACK = ((320, 64, (1, 1)), (384, 64, (1, -1)), (192, 128, (1, 0)), (0, 128, (0, 1)), (128, 64, (0, -1)))


def combine_kernel(sums, cells, dens, lap, got, own_cells, s1, r1, fsem):
    greet([(0, -1), (0, 1), (-1, 0), (-1, -1), (-1, 1)])
    fetch = pltpu.make_async_copy(cells.at[pl.ds(0, 256)], own_cells, fsem)
    fetch.start()
    copies = []
    for k, (row, rows, where) in enumerate(BACK):
        c = copy_to(sums.at[:, pl.ds(256 + row, rows)], got.at[:, pl.ds(row, rows)], s1.at[k], r1.at[k], where)
        c.start()
        copies.append(c)
    x0, _ = centre()
    fetch.wait()
    for c in copies:
        c.wait()
    own = lax.rsqrt(jnp.full((64, 128), 0.01, f32)) - 1.0
    lists = ((0, 192, 320), (256, 384), (64,), (128,))
    for q in range(4):
        rows = slice(64 * q, 64 * q + 64)
        n = sums[0, rows, :]
        s = sums[1, rows, :]
        for r in lists[q]:
            n = n + got[0, r:r + 64, :]
            s = s + got[1, r:r + 64, :]
        filled = own_cells[rows, 0:128] - x0 < 0.5 * SENT
        dens[rows, :] = jnp.where(filled, (n - own) / ref_density, 0.0)
        lap[rows, :] = jnp.where(filled, (s - own_cells[rows, 384:512] * n) / ref_density, 0.0)


def combine(sums, cells):
    vm = pl.BlockSpec(memory_space=pltpu.VMEM)
    return pl.pallas_call(
        combine_kernel,
        out_shape=[jax.ShapeDtypeStruct((256, 128), f32)] * 2,
        in_specs=[vm, pl.BlockSpec(memory_space=pl.ANY)], out_specs=[vm] * 2,
        scratch_shapes=[pltpu.VMEM((2, 448, 128), f32), pltpu.VMEM((256, 512), f32), pltpu.SemaphoreType.DMA((5,)), pltpu.SemaphoreType.DMA((5,)),
                        pltpu.SemaphoreType.DMA],
        compiler_params=pltpu.CompilerParams(collective_id=1, has_side_effects=True, vmem_limit_bytes=16 * 2**20),
        name="combine",
    )(sums, cells)


def local(incoming, dest, counts):
    cells = relayout(incoming.reshape(1024, 128), dest, counts)
    sums = compute(counts, cells)
    density, laplace = combine(sums, cells)
    return density.reshape(2, 2, 64, 128), laplace.reshape(2, 2, 64, 128)


def solution(mesh):
    in_specs = (P("slab", "dom", None, None), P("slab", "dom"), P("slab", "dom", None))
    out_specs = (P("slab", "dom", None, None), P("slab", "dom", None, None))
    return jax.shard_map(local, mesh=mesh, in_specs=in_specs, out_specs=out_specs, check_vma=False)
```
